32 devices in a mesh: dp: 4 (over y, core), ctx: 8 (over z, x).
Axes of the slice: x: 2, y: 2, z: 4, core: 2. Of those that a mesh axis runs over, the one named last changes fastest.
Arguments:
- out_gate: bfloat16 [4, 2048, 512], P('dp', 'ctx'), may hold values from -6 to 6
- key_gate: bfloat16 [4, 2048, 512], P('dp', 'ctx'), may hold values from -6 to 6
- value_input: bfloat16 [4, 2048, 512], P('dp', 'ctx'), may hold values from -6 to 6
- filter_taps: bfloat16 [2048, 512], P('ctx'), may hold values from -2 to 2
- cotangent: bfloat16 [4, 2048, 512], P('dp', 'ctx'), may hold values from -6 to 6
- block_live: int32 [4, 32], P('dp', 'ctx'), may hold values 0 or 1
Outputs:
- grad_out_gate: bfloat16 [4, 2048, 512], P('dp', 'ctx')
- grad_key_gate: bfloat16 [4, 2048, 512], P('dp', 'ctx')
- grad_value: bfloat16 [4, 2048, 512], P('dp', 'ctx')
- grad_taps: bfloat16 [2048, 512], P('ctx')
The draws below stay inside these ranges and needn't reach their ends.
Inputs may be any that keep to these rules, and one draw needn't show every extreme that they name: `block_live`: 1 where a block of 64 tokens holds sequence data, 0 where it is padding.
All inputs are finite; a program needn't handle non-finite values.
Results may differ from the reference program's by a relative error of at most 0.027.
Values may be sent and summed in bfloat16 or wider, within the bound.
No kernel may reach another device: no remote copies, remote signals or barrier semaphores. Data moves between devices by JAX's collectives and lax.ppermute only.
A program may use at most 64 MiB of HBM per device.

```python
import math
import jax
import jax.numpy as jnp
from jax import lax

CH = 512
QLEN = 64
BLOCK = 64
SEQ = 2048
PLEN = 64
BATCH = 4


def draw_filter_taps(key, part):
    rate_key, noise_key = jax.random.split(key)
    lowest = math.log(0.3)
    highest = math.log(SEQ / 30.0)
    decay_rates = jnp.exp(jax.random.uniform(rate_key, (1, CH), jnp.float32, lowest, highest))
    positions = jnp.arange(SEQ, dtype=jnp.float32)[:, None]
    envelope = jnp.exp(-decay_rates * positions / SEQ)
    energy = jnp.expm1(-2.0 * decay_rates) / jnp.expm1(-2.0 * decay_rates / SEQ)
    noise_vals = jnp.clip(jax.random.normal(noise_key, (SEQ, CH), jnp.float32), -6.0, 6.0)
    return (noise_vals * envelope / jnp.sqrt(energy)).astype(jnp.bfloat16)


def set_ends(entries, own_key, smallest, high):
    longest = entries.shape.index(max(entries.shape))
    spots = []
    for shift in (0, 1):
        where = [jax.random.randint(jax.random.fold_in(own_key, axis), (), 0, length) for axis, length in enumerate(entries.shape)]
        where[longest] = (where[longest] + shift) % entries.shape[longest]
        spots.append(tuple(where))
    return entries.at[spots[0]].set(smallest).at[spots[1]].set(high)


def block_levels(rng, extent, cuts, low, top_value):
    def one(dim, parts):
        steps = jax.random.uniform(jax.random.fold_in(jax.random.fold_in(rng, 6), dim), (parts,), jnp.float32, low / len(cuts), top_value / len(cuts))
        return jnp.repeat(jnp.exp(steps), extent[dim] // parts).reshape((-1,) + (1,) * (len(extent) - dim - 1))

    loudness = one(*cuts[0])
    for cut in cuts[1:]:
        loudness = loudness * one(*cut)
    return loudness


def normal_values(own_key, shape, deviation, most, shards=(), held_as=jnp.bfloat16):
    level = block_levels(own_key, shape, shards, -0.22, 0.18) if shards else 1.0
    result = jax.random.normal(own_key, shape, jnp.float32) * deviation * level
    return jnp.minimum(jnp.maximum(result, -most), most).astype(held_as)


def setup_inputs(seed: int = 0) -> dict:
    key_of = jax.random.split(jax.random.key(seed), 7)
    return {
        "out_gate": normal_values(key_of[0], (BATCH, SEQ, CH), 1.0, 6.0, ((0, 4), (1, 8))),
        "key_gate": normal_values(key_of[1], (BATCH, SEQ, CH), 1.0, 6.0, ((0, 4), (1, 8))),
        "value_input": normal_values(key_of[2], (BATCH, SEQ, CH), 1.0, 6.0, ((0, 4), (1, 8))),
        "filter_taps": draw_filter_taps(jax.random.fold_in(key_of[6], 71), 0),
        "cotangent": normal_values(key_of[4], (BATCH, SEQ, CH), 1.0, 6.0, ((0, 4), (1, 8))),
        "block_live": set_ends((jax.random.randint(key_of[5], (BATCH, SEQ // BLOCK), 0, 4) < 3).astype(jnp.int32), jax.random.fold_in(key_of[5], 1), 0, 1),
    }


TWO_PI = 2.0 * math.pi

def angle_table(row_count, col_count, row_start, col_start, period_len, direction):
    row_ids = jnp.arange(row_count, dtype=jnp.int32)[:, None] + row_start
    col_ids = jnp.arange(col_count, dtype=jnp.int32)[None, :] + col_start
    phases = (row_ids * col_ids % period_len).astype(jnp.float32)
    return direction * TWO_PI * phases / period_len

def rounded(values):
    return lax.optimization_barrier(values.astype(jnp.bfloat16)).astype(jnp.float32)

def factor_tables(angles):
    return (rounded(jnp.cos(angles)), rounded(jnp.sin(angles)))

def product(form, left_op, right_op):
    return jnp.einsum(form, left_op, right_op, precision=lax.Precision.HIGHEST)

def forward_full(signal):
    half_rows = PLEN // 2
    total_len = PLEN * QLEN
    grid_values = signal.astype(jnp.float32).reshape(half_rows, QLEN, CH)
    cos_rows, sin_rows = factor_tables(angle_table(PLEN, half_rows, 0, 0, PLEN, -1.0))
    real_part = product('kp,pqc->kqc', cos_rows, grid_values)
    imag_part = product('kp,pqc->kqc', sin_rows, grid_values)
    twist_angles = angle_table(PLEN, QLEN, 0, 0, total_len, -1.0)
    turn_cos = jnp.cos(twist_angles)[:, :, None]
    turn_sin = jnp.sin(twist_angles)[:, :, None]
    real_twist = rounded(real_part * turn_cos - imag_part * turn_sin)
    imag_twist = rounded(real_part * turn_sin + imag_part * turn_cos)
    cos_cols, sin_cols = factor_tables(angle_table(QLEN, QLEN, 0, 0, QLEN, -1.0))
    real_out = product('aqc,qk->akc', real_twist, cos_cols) - product('aqc,qk->akc', imag_twist, sin_cols)
    imag_out = product('aqc,qk->akc', real_twist, sin_cols) + product('aqc,qk->akc', imag_twist, cos_cols)
    return (rounded(real_out), rounded(imag_out))

def inverse_full(real_in, imag_in):
    total_len = PLEN * QLEN
    cos_cols, sin_cols = factor_tables(angle_table(QLEN, QLEN, 0, 0, QLEN, 1.0))
    real_part = product('akc,kq->aqc', real_in, cos_cols) - product('akc,kq->aqc', imag_in, sin_cols)
    imag_part = product('akc,kq->aqc', real_in, sin_cols) + product('akc,kq->aqc', imag_in, cos_cols)
    twist_angles = angle_table(PLEN, QLEN, 0, 0, total_len, 1.0)
    turn_cos = jnp.cos(twist_angles)[:, :, None]
    turn_sin = jnp.sin(twist_angles)[:, :, None]
    real_twist = rounded(real_part * turn_cos - imag_part * turn_sin)
    imag_twist = rounded(real_part * turn_sin + imag_part * turn_cos)
    cos_back, sin_back = factor_tables(angle_table(PLEN // 2, PLEN, 0, 0, PLEN, 1.0))
    signal = product('pk,kqc->pqc', cos_back, real_twist) - product('pk,kqc->pqc', sin_back, imag_twist)
    return (signal * (1.0 / total_len)).astype(jnp.bfloat16).reshape(SEQ, CH)

def spectrum_product(left_real, left_imag, right_real, right_imag, conjugate):
    if conjugate:
        real_out = left_real * right_real + left_imag * right_imag
        imag_out = left_imag * right_real - left_real * right_imag
    else:
        real_out = left_real * right_real - left_imag * right_imag
        imag_out = left_real * right_imag + left_imag * right_real
    return (rounded(real_out), rounded(imag_out))

def reference(out_gate, key_gate, value_input, filter_taps, cotangent, block_live):
    filter_real, filter_imag = forward_full(filter_taps)
    live_tokens = jnp.repeat(block_live.astype(jnp.float32), BLOCK, axis=1)[:, :, None]

    def one_sequence(taps_total, row_items):
        gate_row, key_row, value_row, cot_row, live_row = row_items
        key_wide = key_row.astype(jnp.float32)
        value_wide = value_row.astype(jnp.float32)
        cot_wide = cot_row.astype(jnp.float32)
        gated_input = (key_wide * value_wide * live_row).astype(jnp.bfloat16)
        back_signal = (cot_wide * gate_row.astype(jnp.float32)).astype(jnp.bfloat16)
        fwd_real, fwd_imag = forward_full(gated_input)
        back_real, back_imag = forward_full(back_signal)
        conv_real, conv_imag = spectrum_product(fwd_real, fwd_imag, filter_real, filter_imag, False)
        conv_out = inverse_full(conv_real, conv_imag)
        grad_real, grad_imag = spectrum_product(back_real, back_imag, filter_real, filter_imag, True)
        grad_conv = inverse_full(grad_real, grad_imag)
        taps_real, taps_imag = spectrum_product(back_real, back_imag, fwd_real, fwd_imag, True)
        taps_seq = inverse_full(taps_real, taps_imag)
        grad_gate = (cot_wide * conv_out.astype(jnp.float32)).astype(jnp.bfloat16)
        grad_wide = grad_conv.astype(jnp.float32)
        grad_key = (grad_wide * value_wide * live_row).astype(jnp.bfloat16)
        grad_value = (grad_wide * key_wide * live_row).astype(jnp.bfloat16)
        return (taps_total + taps_seq.astype(jnp.float32), (grad_gate, grad_key, grad_value))
    taps_total, grad_rows = lax.scan(one_sequence, jnp.zeros((SEQ, CH), jnp.float32), (out_gate, key_gate, value_input, cotangent, live_tokens))
    grad_taps = (taps_total * (1.0 / math.sqrt(BATCH * SEQ))).astype(jnp.bfloat16)
    return (grad_rows[0], grad_rows[1], grad_rows[2], grad_taps)
```

```python
import functools
import math

import jax
import jax.numpy as jnp
import ml_dtypes
import numpy as np
from jax import lax
from jax.experimental import pallas as pl
from jax.experimental.pallas import tpu as pltpu
from jax.sharding import PartitionSpec as P


SUB = 8
VMEM = 60 * 1024 * 1024
F32 = jnp.float32
BF16 = jnp.bfloat16


def transform_tables(prow, qlen):
    total = prow * qlen
    k1 = np.arange(prow)
    p = np.arange(prow)
    theta = 2.0 * np.pi * (((4 * k1[:, None] + 1) * p[None, :]) % (4 * prow)) / (4 * prow)
    eye = np.eye(SUB)
    first = np.stack([np.cos(theta), -np.sin(theta)], axis=1)
    first = np.einsum("krp,ab->krapb", first, eye).reshape(prow * 2 * SUB, prow * SUB)
    last = np.stack([np.cos(theta), -np.sin(theta)], axis=0) / total
    last = last.reshape(2, prow // 2, 2, prow)
    last = np.einsum("rmlp,ab->pamrlb", last, eye).reshape(prow * SUB, prow * 2 * SUB)
    q = np.arange(qlen)
    k2 = np.arange(qlen)
    phase = (4 * k1[:, None, None] + 1 + 4 * prow * k2[None, :, None]) * q[None, None, :]
    phi = 2.0 * np.pi * (phase % (4 * total)) / (4 * total)
    re, im = np.cos(phi), -np.sin(phi)
    mid = np.concatenate(
        [np.concatenate([re, -im], axis=2), np.concatenate([im, re], axis=2)], axis=1
    )
    back = np.swapaxes(mid, 1, 2)
    return [t.astype(ml_dtypes.bfloat16) for t in (first, mid, back, last)]


def dot(a, b):
    return jnp.dot(a, b, preferred_element_type=F32)


def prep_kernel(core, live, out_gate, key, value, cot, taps, out):
    groups = out.shape[0]
    share = out.shape[2] // 2
    blocks = live.shape[1]
    tok = key.shape[1]
    qlen = tok // blocks
    qblocks = qlen // SUB
    for p in range(0, blocks, 2):
        pair = []
        for e in (0, 1):
            rows = slice((p + e) * qlen, (p + e + 1) * qlen)
            alive = live[0, p + e].astype(F32)
            u = key[0, rows, :].astype(F32) * value[0, rows, :].astype(F32) * alive
            g = cot[0, rows, :].astype(F32) * out_gate[0, rows, :].astype(F32)
            pair.append((u, g))
        for j in range(groups):
            lanes = slice(j * share, (j + 1) * share)
            ends = [
                jnp.concatenate([u[:, lanes], g[:, lanes]], axis=1).reshape(qblocks, 1, SUB, 2 * share)
                for u, g in pair
            ]
            both = jnp.concatenate(ends, axis=1).reshape(qblocks, 2 * SUB, 2 * share).astype(BF16)
            for qb in range(qblocks):
                start = qb * blocks * SUB + p * SUB
                out[j, start : start + 2 * SUB, :] = both[qb]
    half = tok // 2
    mine = taps[pl.ds(pl.multiple_of(core[0] * half, half), half), :].astype(F32)
    for j in range(groups):
        lanes = slice(j * share, (j + 1) * share)
        both = jnp.concatenate([mine[:qlen, lanes], mine[qlen:, lanes]], axis=1)
        out[j, tok:, :] = both.astype(BF16)


def stage_one(first, load, rows, qblocks, dest):
    width = dest.shape[2]
    pairs = dest.shape[0]
    for qb in range(0, qblocks, 2):
        ends = [
            dot(first[...], load(qb + e)).reshape(pairs, SUB, width) for e in (0, 1)
        ]
        dest[:, qb * SUB : (qb + 2) * SUB, :] = jnp.concatenate(ends, axis=1).astype(BF16)


def store_pair(ends, m, qblocks, held):
    width = held.shape[2]
    parts = [e.reshape(2, qblocks, 1, SUB, width) for e in ends]
    both = jnp.concatenate(parts, axis=2).reshape(2, qblocks, 2 * SUB, width).astype(BF16)
    for qb in range(qblocks):
        for r in (0, 1):
            start = pl.multiple_of(m * 4 * SUB + r * 2 * SUB, 2 * SUB)
            held[qb, pl.ds(start, 2 * SUB), :] = both[r, qb]


def signs(shape, share):
    lane = lax.broadcasted_iota(jnp.int32, shape, 1)
    return lane < share


def swap(x, share):
    return jnp.concatenate([x[:, share:], x[:, :share]], axis=1)


def taps_kernel(core, recv, first, mid, back, last, spec, keep, send, rows_held, held):
    groups, _, width = recv.shape
    share = width // 2
    prow = mid.shape[0]
    qlen = mid.shape[1] // 2
    qblocks = qlen // SUB
    each = prow // groups * SUB

    def load(qb):
        return recv[:, qb * each : (qb + 1) * each, :].reshape(groups * each, width)

    stage_one(first, load, prow, qblocks, rows_held)
    low = signs((qlen, width), share)

    def step(m, carry):
        ends = []
        for e in (0, 1):
            k1 = 2 * m + e
            rows = rows_held[pl.ds(2 * k1, 2)].reshape(2 * qlen, width)
            full = dot(mid[k1], rows)
            spec[k1] = full.astype(BF16)
            re, im = full[:qlen], full[qlen:]
            ore, oim = swap(re, share), swap(im, share)
            tre = re * ore + im * oim
            tim = im * ore - re * oim
            tim = jnp.where(low, -tim, tim)
            both = jnp.concatenate([tre, tim], axis=0).astype(BF16)
            ends.append(dot(back[k1], both))
        store_pair(ends, m, qblocks, held)
        return carry

    lax.fori_loop(0, prow // 2, step, 0, unroll=4)
    blocks = prow // groups
    flip = core[0] == 0
    low_tile = signs((SUB, width), share)
    for qb in range(0, qblocks, 2):
        halves = [[], []]
        for e in (0, 1):
            seq = dot(last[...], held[qb + e]).reshape(groups, blocks, SUB, width)
            for c in (0, 1):
                halves[c].append(jnp.where(low_tile, seq[:, 2 * c], seq[:, 2 * c + 1]))
        a, b = [jnp.concatenate(h, axis=1) for h in halves]
        rows = slice(qb * SUB, (qb + 2) * SUB)
        keep[:, rows, :] = jnp.where(flip, a, b).astype(BF16)
        send[:, rows, :] = jnp.where(flip, b, a).astype(BF16)


def main_kernel(core, recv, other, spec, first, mid, back, last, out, taps_held, rows_held, held):
    groups, full_rows, width = recv.shape
    share = width // 2
    prow = mid.shape[0]
    qlen = mid.shape[1] // 2
    qblocks = qlen // SUB
    blocks = prow // groups
    each = blocks * SUB
    tok = blocks * qlen
    flip = core[0] == 0

    def unpack(i, carry):
        mine = recv[i, tok:, :].astype(F32)
        theirs = other[i].astype(F32)
        for c in (0, 1):
            x = jnp.where(flip == (c == 0), mine, theirs)
            lo, hi = x[:, :share], x[:, share:]
            ends = [
                jnp.concatenate([h, h], axis=1).reshape(qblocks, 1, SUB, width) for h in (lo, hi)
            ]
            both = jnp.concatenate(ends, axis=1).reshape(qblocks, 2 * SUB, width).astype(BF16)
            for qb in range(qblocks):
                start = pl.multiple_of(i * each + c * 2 * SUB, 2 * SUB)
                taps_held[qb, pl.ds(start, 2 * SUB), :] = both[qb]
        return carry

    lax.fori_loop(0, groups, unpack, 0, unroll=8)
    stage_one(first, lambda qb: taps_held[qb], prow, qblocks, rows_held)
    low = signs((qlen, width), share)

    def step(m, carry):
        ends = []
        for e in (0, 1):
            k1 = 2 * m + e
            rows = rows_held[pl.ds(2 * k1, 2)].reshape(2 * qlen, width)
            filt = dot(mid[k1], rows)
            hre, him = filt[:qlen], filt[qlen:]
            him = jnp.where(low, him, -him)
            sig = spec[k1].astype(F32)
            re, im = sig[:qlen], sig[qlen:]
            both = jnp.concatenate([re * hre - im * him, re * him + im * hre], axis=0)
            ends.append(dot(back[k1], both.astype(BF16)))
        store_pair(ends, m, qblocks, held)
        return carry

    lax.fori_loop(0, prow // 2, step, 0, unroll=4)
    for qb in range(qblocks):
        seq = dot(last[...], held[qb]).reshape(groups, each, width)
        out[:, qb * each : (qb + 1) * each, :] = seq.astype(BF16)


def add_kernel(a, b, out):
    out[...] = (a[...].astype(F32) + b[...].astype(F32)).astype(BF16)


def join_kernel(a, b, whole, out):
    total = (a[...].astype(F32) + b[...].astype(F32)).astype(BF16)
    out[...] = total


def post_kernel(live, recv, key, value, cot, gate_out, key_out, value_out):
    groups, _, width = recv.shape
    share = width // 2
    blocks = live.shape[1]
    tok = key.shape[1]
    qlen = tok // blocks
    qblocks = qlen // SUB
    parts = [
        recv[j, :tok, :].astype(F32).reshape(qblocks, blocks, SUB, width) for j in range(groups)
    ]
    for p in range(blocks):
        rows = slice(p * qlen, (p + 1) * qlen)
        alive = live[0, p].astype(F32)
        mine = [x[:, p].reshape(qlen, width) for x in parts]
        conv = jnp.concatenate([x[:, :share] for x in mine], axis=1)
        grad = jnp.concatenate([x[:, share:] for x in mine], axis=1)
        gate_out[0, rows, :] = (cot[0, rows, :].astype(F32) * conv).astype(BF16)
        key_out[0, rows, :] = (grad * value[0, rows, :].astype(F32) * alive).astype(BF16)
        value_out[0, rows, :] = (grad * key[0, rows, :].astype(F32) * alive).astype(BF16)


def finish_kernel(scale, core, mine, theirs, out):
    groups, qlen, width = mine.shape
    share = width // 2
    flip = core[0] == 0
    a = mine[...].astype(F32) * scale
    b = theirs[...].astype(F32) * scale
    for c in (0, 1):
        x = jnp.where(flip == (c == 0), a, b)
        for e in (0, 1):
            row = jnp.concatenate(
                [x[j][:, e * share : (e + 1) * share] for j in range(groups)], axis=1
            )
            start = (2 * c + e) * qlen
            out[start : start + qlen, :] = row.astype(BF16)


SMEM = pl.BlockSpec(memory_space=pltpu.SMEM)
VM = pl.BlockSpec(memory_space=pltpu.VMEM)


def call(kernel, ins, outs, scratch=(), aliases=None, smem=0, name=None, flops=0, out_specs=None, in_specs=None):
    nbytes = sum(math.prod(x.shape) * 2 for x in ins) + sum(math.prod(x.shape) * 2 for x in outs)
    return pl.pallas_call(
        kernel,
        out_shape=outs if len(outs) > 1 else outs[0],
        in_specs=in_specs or ([SMEM] * smem + [VM] * (len(ins) - smem)),
        out_specs=out_specs or ([VM] * len(outs) if len(outs) > 1 else VM),
        scratch_shapes=list(scratch),
        input_output_aliases=aliases or {},
        compiler_params=pltpu.CompilerParams(vmem_limit_bytes=VMEM),
        cost_estimate=pl.CostEstimate(flops=flops, bytes_accessed=nbytes, transcendentals=0),
        name=name,
    )(*ins)


def shaped(shape, dtype=BF16):
    return jax.ShapeDtypeStruct(shape, dtype)


def local(out_gate, key_gate, value_input, filter_taps, cotangent, block_live):
    ctx = lax.axis_size("ctx")
    dp = lax.axis_size("dp")
    tok, chans = key_gate.shape[1:]
    blocks = block_live.shape[1]
    qlen = tok // blocks
    prow = blocks * ctx
    share = chans // ctx
    width = 2 * share
    qblocks = qlen // SUB
    tables = [jnp.asarray(t) for t in transform_tables(prow, qlen)]
    core = (lax.axis_index("dp") % 2).astype(jnp.int32).reshape(1)

    def trade(x, bit):
        return lax.ppermute(x, "dp", [(i, i ^ bit) for i in range(dp)])

    packed = call(
        prep_kernel,
        [core, block_live, out_gate, key_gate, value_input, cotangent, filter_taps],
        [shaped((ctx, tok + qlen, width))],
        smem=2,
        name="gate_and_pack",
    )
    recv = lax.all_to_all(packed, "ctx", split_axis=0, concat_axis=0, tiled=True)
    other_taps = trade(recv[:, tok:, :], 1)
    spec, keep, send = call(
        taps_kernel,
        [core, recv, *tables],
        [shaped((prow, 2 * qlen, width))] + [shaped((ctx, qlen, width))] * 2,
        scratch=[
            pltpu.VMEM((2 * prow, qlen, width), BF16),
            pltpu.VMEM((qblocks, 2 * prow * SUB, width), BF16),
        ],
        smem=1,
        name="taps_gradient",
    )
    got = trade(send, 1)
    outs = call(
        main_kernel,
        [core, recv, other_taps, spec, *tables],
        [shaped((ctx, tok + qlen, width))],
        scratch=[
            pltpu.VMEM((qblocks, prow * SUB, width), BF16),
            pltpu.VMEM((2 * prow, qlen, width), BF16),
            pltpu.VMEM((qblocks, 2 * prow * SUB, width), BF16),
        ],
        smem=1,
        name="convolve",
    )
    total = call(add_kernel, [keep, got], [shaped(keep.shape)], name="add_core")
    bit = 2
    while bit < dp:
        got = trade(total, bit)
        bit *= 2
        if bit < dp:
            total = call(add_kernel, [total, got], [shaped(keep.shape)], name="add_chip")
    summed = (total.astype(F32) + got.astype(F32)).astype(BF16)
    back = lax.dynamic_update_slice(outs, summed, (0, tok, 0))
    recv = lax.all_to_all(back, "ctx", split_axis=0, concat_axis=0, tiled=True)
    mine = recv[:, tok:, :]
    theirs = trade(mine, 1)
    grads = call(
        post_kernel,
        [block_live, recv, key_gate, value_input, cotangent],
        [shaped(key_gate.shape)] * 3,
        smem=1,
        name="ungate",
    )
    scale = 1.0 / math.sqrt(dp * tok * ctx)
    grad_taps = call(
        functools.partial(finish_kernel, scale),
        [core, mine, theirs],
        [shaped(filter_taps.shape)],
        smem=1,
        name="scale_taps",
    )
    return (*grads, grad_taps)


def solution(mesh):
    return jax.shard_map(
        local,
        mesh=mesh,
        in_specs=(
            P("dp", "ctx", None),
            P("dp", "ctx", None),
            P("dp", "ctx", None),
            P("ctx", None),
            P("dp", "ctx", None),
            P("dp", "ctx"),
        ),
        out_specs=(
            P("dp", "ctx", None),
            P("dp", "ctx", None),
            P("dp", "ctx", None),
            P("ctx", None),
        ),
        check_vma=False,
    )
```

```python
import functools
import math

import jax
import jax.numpy as jnp
import ml_dtypes
import numpy as np
from jax import lax
from jax.experimental import pallas as pl
from jax.experimental.pallas import tpu as pltpu
from jax.sharding import PartitionSpec as P


SUB = 8
SPARE = 4 * 1024 * 1024
F32 = jnp.float32
BF16 = jnp.bfloat16


def transform_tables(prow, qlen):
    total = prow * qlen
    k1 = np.arange(prow)
    p = np.arange(prow)
    theta = 2.0 * np.pi * (((4 * k1[:, None] + 1) * p[None, :]) % (4 * prow)) / (4 * prow)
    eye = np.eye(SUB)
    first = np.stack([np.cos(theta), -np.sin(theta)], axis=1)
    first = np.einsum("krp,ab->krapb", first, eye).reshape(prow * 2 * SUB, prow * SUB)
    last = np.stack([np.cos(theta), -np.sin(theta)], axis=0) / total
    last = last.reshape(2, prow // 2, 2, prow)
    last = np.einsum("rmlp,ab->pamrlb", last, eye).reshape(prow * SUB, prow * 2 * SUB)
    q = np.arange(qlen)
    k2 = np.arange(qlen)
    phase = (4 * k1[:, None, None] + 1 + 4 * prow * k2[None, :, None]) * q[None, None, :]
    phi = 2.0 * np.pi * (phase % (4 * total)) / (4 * total)
    re, im = np.cos(phi), -np.sin(phi)
    mid = np.concatenate(
        [np.concatenate([re, -im], axis=2), np.concatenate([im, re], axis=2)], axis=1
    )
    back = np.swapaxes(mid, 1, 2)
    return [t.astype(ml_dtypes.bfloat16) for t in (first, mid, back, last)]


def dot(a, b):
    return jnp.dot(a, b, preferred_element_type=F32)


def core_place():
    return lax.rem(lax.axis_index("dp"), 2)


def prep_kernel(
    live_far, out_gate_far, key_far, value_far, cot_far, taps_far,
    out, key_out, value_out, cot, key, value, out_gate, taps, live, sems,
):
    core = core_place()
    groups = out.shape[0]
    share = out.shape[2] // 2
    blocks = live.shape[1]
    tok = key.shape[0]
    qlen = tok // blocks
    qblocks = qlen // SUB
    copies = []
    for p in range(0, blocks, 2):
        rows = slice(p * qlen, (p + 2) * qlen)
        copies.append([
            pltpu.make_async_copy(far.at[0, rows], near.at[rows], sems.at[2 * p + i])
            for i, (far, near) in enumerate(
                [(key_far, key), (value_far, value), (cot_far, cot), (out_gate_far, out_gate)]
            )
        ])
    half = tok // 2
    taps_copy = pltpu.make_async_copy(
        taps_far.at[pl.ds(pl.multiple_of(core * half, half), half)], taps, sems.at[2 * blocks]
    )
    live_copy = pltpu.make_async_copy(live_far, live, sems.at[2 * blocks + 1])
    live_copy.start()
    for group in copies:
        for copy in group:
            copy.start()
    taps_copy.start()
    live_copy.wait()
    for p in range(0, blocks, 2):
        for copy in copies[p // 2]:
            copy.wait()
        pair = []
        for e in (0, 1):
            rows = slice((p + e) * qlen, (p + e + 1) * qlen)
            alive = live[0, p + e].astype(F32)
            kept = key[rows, :].astype(F32) * alive
            u = kept * value[rows, :].astype(F32)
            key_out[rows, :] = kept.astype(BF16)
            value_out[rows, :] = (value[rows, :].astype(F32) * alive).astype(BF16)
            g = cot[rows, :].astype(F32) * out_gate[rows, :].astype(F32)
            pair.append((u, g))
        for j in range(groups):
            lanes = slice(j * share, (j + 1) * share)
            ends = [
                jnp.concatenate([u[:, lanes], g[:, lanes]], axis=1).reshape(qblocks, 1, SUB, 2 * share)
                for u, g in pair
            ]
            both = jnp.concatenate(ends, axis=1).reshape(qblocks, 2 * SUB, 2 * share).astype(BF16)
            for qb in range(qblocks):
                start = qb * blocks * SUB + p * SUB
                out[j, start : start + 2 * SUB, :] = both[qb]
    taps_copy.wait()
    mine = taps[...].astype(F32)
    for j in range(groups):
        lanes = slice(j * share, (j + 1) * share)
        both = jnp.concatenate([mine[:qlen, lanes], mine[qlen:, lanes]], axis=1)
        out[j, tok:, :] = both.astype(BF16)


def stage_one(first, load, rows, qblocks, dest):
    width = dest.shape[2]
    pairs = dest.shape[0]
    for qb in range(0, qblocks, 2):
        ends = [
            dot(first[...], load(qb + e)).reshape(pairs, SUB, width) for e in (0, 1)
        ]
        dest[:, qb * SUB : (qb + 2) * SUB, :] = jnp.concatenate(ends, axis=1).astype(BF16)


def store_pair(ends, m, qblocks, held):
    width = held.shape[2]
    parts = [e.reshape(2, qblocks, 1, SUB, width) for e in ends]
    both = jnp.concatenate(parts, axis=2).reshape(2, qblocks, 2 * SUB, width).astype(BF16)
    for qb in range(qblocks):
        for r in (0, 1):
            start = pl.multiple_of(m * 4 * SUB + r * 2 * SUB, 2 * SUB)
            held[qb, pl.ds(start, 2 * SUB), :] = both[r, qb]


def signs(shape, share):
    lane = lax.broadcasted_iota(jnp.int32, shape, 1)
    return lane < share


def swap(x, share):
    return jnp.concatenate([x[:, share:], x[:, :share]], axis=1)


def taps_kernel(recv, first, mid, back, last, spec, keep, send, rows_held, held):
    groups, _, width = recv.shape
    share = width // 2
    prow = mid.shape[0]
    qlen = mid.shape[1] // 2
    qblocks = qlen // SUB
    each = prow // groups * SUB

    def load(qb):
        return recv[:, qb * each : (qb + 1) * each, :].reshape(groups * each, width)

    stage_one(first, load, prow, qblocks, rows_held)
    low = signs((qlen, width), share)

    def step(m, carry):
        ends = []
        for e in (0, 1):
            k1 = 2 * m + e
            rows = rows_held[pl.ds(2 * k1, 2)].reshape(2 * qlen, width)
            full = dot(mid[k1], rows)
            spec[k1] = full.astype(BF16)
            re, im = full[:qlen], full[qlen:]
            ore, oim = swap(re, share), swap(im, share)
            tre = re * ore + im * oim
            tim = im * ore - re * oim
            tim = jnp.where(low, -tim, tim)
            both = jnp.concatenate([tre, tim], axis=0).astype(BF16)
            ends.append(dot(back[k1], both))
        store_pair(ends, m, qblocks, held)
        return carry

    lax.fori_loop(0, prow // 2, step, 0, unroll=4)
    blocks = prow // groups
    flip = core_place() == 0
    low_tile = signs((SUB, width), share)
    for qb in range(0, qblocks, 2):
        halves = [[], []]
        for e in (0, 1):
            seq = dot(last[...], held[qb + e]).reshape(groups, blocks, SUB, width)
            for c in (0, 1):
                halves[c].append(jnp.where(low_tile, seq[:, 2 * c], seq[:, 2 * c + 1]))
        a, b = [jnp.concatenate(h, axis=1) for h in halves]
        rows = slice(qb * SUB, (qb + 2) * SUB)
        keep[:, rows, :] = jnp.where(flip, a, b).astype(BF16)
        send[:, rows, :] = jnp.where(flip, b, a).astype(BF16)


def main_kernel(recv, other, spec, first, mid, back, last, out, taps_held, rows_held, held):
    groups, full_rows, width = recv.shape
    share = width // 2
    prow = mid.shape[0]
    qlen = mid.shape[1] // 2
    qblocks = qlen // SUB
    blocks = prow // groups
    each = blocks * SUB
    tok = blocks * qlen
    flip = core_place() == 0

    def unpack(i, carry):
        mine = recv[i, tok:, :].astype(F32)
        theirs = other[i].astype(F32)
        for c in (0, 1):
            x = jnp.where(flip == (c == 0), mine, theirs)
            lo, hi = x[:, :share], x[:, share:]
            ends = [
                jnp.concatenate([h, h], axis=1).reshape(qblocks, 1, SUB, width) for h in (lo, hi)
            ]
            both = jnp.concatenate(ends, axis=1).reshape(qblocks, 2 * SUB, width).astype(BF16)
            for qb in range(qblocks):
                start = pl.multiple_of(i * each + c * 2 * SUB, 2 * SUB)
                taps_held[qb, pl.ds(start, 2 * SUB), :] = both[qb]
        return carry

    lax.fori_loop(0, groups, unpack, 0, unroll=8)
    stage_one(first, lambda qb: taps_held[qb], prow, qblocks, rows_held)
    low = signs((qlen, width), share)

    def step(m, carry):
        ends = []
        for e in (0, 1):
            k1 = 2 * m + e
            rows = rows_held[pl.ds(2 * k1, 2)].reshape(2 * qlen, width)
            filt = dot(mid[k1], rows)
            hre, him = filt[:qlen], filt[qlen:]
            him = jnp.where(low, him, -him)
            sig = spec[k1].astype(F32)
            re, im = sig[:qlen], sig[qlen:]
            both = jnp.concatenate([re * hre - im * him, re * him + im * hre], axis=0)
            ends.append(dot(back[k1], both.astype(BF16)))
        store_pair(ends, m, qblocks, held)
        return carry

    lax.fori_loop(0, prow // 2, step, 0, unroll=4)
    for qb in range(qblocks):
        seq = dot(last[...], held[qb]).reshape(groups, each, width)
        out[:, qb * each : (qb + 1) * each, :] = seq.astype(BF16)


def add_kernel(a, b, out):
    out[...] = (a[...].astype(F32) + b[...].astype(F32)).astype(BF16)


def post_kernel(
    recv, key, value, cot, gate_far, key_far, value_far, gate_out, key_out, value_out, sems
):
    groups, _, width = recv.shape
    share = width // 2
    tok = key.shape[0]
    qlen = recv.shape[1] - tok
    blocks = tok // qlen
    qblocks = qlen // SUB
    parts = [
        recv[j, :tok, :].astype(F32).reshape(qblocks, blocks, SUB, width) for j in range(groups)
    ]
    copies = []
    for p in range(blocks):
        rows = slice(p * qlen, (p + 1) * qlen)
        mine = [x[:, p].reshape(qlen, width) for x in parts]
        conv = jnp.concatenate([x[:, :share] for x in mine], axis=1)
        grad = jnp.concatenate([x[:, share:] for x in mine], axis=1)
        gate_out[rows, :] = (cot[rows, :].astype(F32) * conv).astype(BF16)
        key_out[rows, :] = (grad * value[rows, :].astype(F32)).astype(BF16)
        value_out[rows, :] = (grad * key[rows, :].astype(F32)).astype(BF16)
        for i, (near, far) in enumerate(
            [(gate_out, gate_far), (key_out, key_far), (value_out, value_far)]
        ):
            copy = pltpu.make_async_copy(near.at[rows], far.at[0, rows], sems.at[3 * p + i])
            copy.start()
            copies.append(copy)
    for copy in copies:
        copy.wait()


def finish_kernel(scale, mine, theirs, out):
    groups, qlen, width = mine.shape
    share = width // 2
    flip = core_place() == 0
    a = mine[...].astype(F32) * scale
    b = theirs[...].astype(F32) * scale
    for c in (0, 1):
        x = jnp.where(flip == (c == 0), a, b)
        for e in (0, 1):
            row = jnp.concatenate(
                [x[j][:, e * share : (e + 1) * share] for j in range(groups)], axis=1
            )
            start = (2 * c + e) * qlen
            out[start : start + qlen, :] = row.astype(BF16)


VM = pl.BlockSpec(memory_space=pltpu.VMEM)
FAR = pl.BlockSpec(memory_space=pltpu.HBM)


def call(kernel, ins, outs, scratch=(), aliases=None, name=None, flops=0, out_specs=None, in_specs=None):
    nbytes = sum(math.prod(x.shape) * 2 for x in [*ins, *outs])
    held = nbytes + sum(math.prod(x.shape) * 2 for x in scratch if x.dtype == BF16)
    return pl.pallas_call(
        kernel,
        out_shape=outs if len(outs) > 1 else outs[0],
        in_specs=in_specs or ([VM] * len(ins)),
        out_specs=out_specs or ([VM] * len(outs) if len(outs) > 1 else VM),
        scratch_shapes=list(scratch),
        input_output_aliases=aliases or {},
        compiler_params=pltpu.CompilerParams(vmem_limit_bytes=held + SPARE),
        cost_estimate=pl.CostEstimate(flops=flops, bytes_accessed=nbytes, transcendentals=0),
        name=name,
    )(*ins)


def shaped(shape, dtype=BF16):
    return jax.ShapeDtypeStruct(shape, dtype)


def local(out_gate, key_gate, value_input, filter_taps, cotangent, block_live):
    ctx = lax.axis_size("ctx")
    dp = lax.axis_size("dp")
    tok, chans = key_gate.shape[1:]
    blocks = block_live.shape[1]
    qlen = tok // blocks
    prow = blocks * ctx
    share = chans // ctx
    width = 2 * share
    qblocks = qlen // SUB
    tables = [jnp.asarray(t) for t in transform_tables(prow, qlen)]
    def trade(x, bit):
        return lax.ppermute(x, "dp", [(i, i ^ bit) for i in range(dp)])

    flat = (tok, chans)
    packed, key, value, cot = call(
        prep_kernel,
        [
            pltpu.with_memory_space_constraint(x, pltpu.HBM)
            for x in (block_live, out_gate, key_gate, value_input, cotangent, filter_taps)
        ],
        [shaped((ctx, tok + qlen, width))] + [shaped(flat)] * 3,
        scratch=[
            *[pltpu.VMEM(flat, BF16)] * 3,
            pltpu.VMEM((tok // 2, chans), BF16),
            pltpu.SMEM(block_live.shape, jnp.int32),
            pltpu.SemaphoreType.DMA((2 * blocks + 2,)),
        ],
        in_specs=[FAR] * 6,
        name="gate_and_pack",
    )
    recv = lax.all_to_all(packed, "ctx", split_axis=0, concat_axis=0, tiled=True)
    other_taps = trade(recv[:, tok:, :], 1)
    spec, keep, send = call(
        taps_kernel,
        [recv, *tables],
        [shaped((prow, 2 * qlen, width))] + [shaped((ctx, qlen, width))] * 2,
        scratch=[
            pltpu.VMEM((2 * prow, qlen, width), BF16),
            pltpu.VMEM((qblocks, 2 * prow * SUB, width), BF16),
        ],
        name="taps_gradient",
    )
    got = trade(send, 1)
    outs = call(
        main_kernel,
        [recv, other_taps, spec, *tables],
        [shaped((ctx, tok + qlen, width))],
        scratch=[
            pltpu.VMEM((qblocks, prow * SUB, width), BF16),
            pltpu.VMEM((2 * prow, qlen, width), BF16),
            pltpu.VMEM((qblocks, 2 * prow * SUB, width), BF16),
        ],
        name="convolve",
    )
    total = call(add_kernel, [keep, got], [shaped(keep.shape)], name="add_core")
    bit = 2
    while bit < dp:
        got = trade(total, bit)
        bit *= 2
        if bit < dp:
            total = call(add_kernel, [total, got], [shaped(keep.shape)], name="add_chip")
    summed = (total.astype(F32) + got.astype(F32)).astype(BF16)
    back = lax.dynamic_update_slice(outs, summed, (0, tok, 0))
    recv = lax.all_to_all(back, "ctx", split_axis=0, concat_axis=0, tiled=True)
    mine = recv[:, tok:, :]
    theirs = trade(mine, 1)
    grads = call(
        post_kernel,
        [recv, key, value, cot],
        [shaped(key_gate.shape)] * 3,
        scratch=[pltpu.VMEM(flat, BF16)] * 3 + [pltpu.SemaphoreType.DMA((3 * blocks,))],
        out_specs=[FAR] * 3,
        name="ungate",
    )
    scale = 1.0 / math.sqrt(dp * tok * ctx)
    grad_taps = call(
        functools.partial(finish_kernel, scale),
        [mine, theirs],
        [shaped(filter_taps.shape)],
        name="scale_taps",
    )
    return (*grads, grad_taps)


def solution(mesh):
    return jax.shard_map(
        local,
        mesh=mesh,
        in_specs=(
            P("dp", "ctx", None),
            P("dp", "ctx", None),
            P("dp", "ctx", None),
            P("ctx", None),
            P("dp", "ctx", None),
            P("dp", "ctx"),
        ),
        out_specs=(
            P("dp", "ctx", None),
            P("dp", "ctx", None),
            P("dp", "ctx", None),
            P("ctx", None),
        ),
        check_vma=False,
    )
```

```python
import functools
import math

import jax
import jax.numpy as jnp
import ml_dtypes
import numpy as np
from jax import lax
from jax.experimental import pallas as pl
from jax.experimental.pallas import tpu as pltpu
from jax.sharding import PartitionSpec as P


SUB = 8
TEAM = 4
PIECES = 4
SPARE = 4 * 1024 * 1024
F32 = jnp.float32
BF16 = jnp.bfloat16


def transform_tables(prow, qlen):
    total = prow * qlen
    k1 = np.arange(prow)
    p = np.arange(prow)
    theta = 2.0 * np.pi * (((4 * k1[:, None] + 1) * p[None, :]) % (4 * prow)) / (4 * prow)
    eye = np.eye(SUB)
    first = np.stack([np.cos(theta), -np.sin(theta)], axis=1)
    first = np.einsum("krp,ab->krapb", first, eye).reshape(prow * 2 * SUB, prow * SUB)
    last = np.stack([np.cos(theta), -np.sin(theta)], axis=0) / total
    last = last.reshape(2, prow // 2, 2, prow)
    last = np.einsum("rmlp,ab->pamrlb", last, eye).reshape(prow * SUB, prow * 2 * SUB)
    q = np.arange(qlen)
    k2 = np.arange(qlen)
    phase = (4 * k1[:, None, None] + 1 + 4 * prow * k2[None, :, None]) * q[None, None, :]
    phi = 2.0 * np.pi * (phase % (4 * total)) / (4 * total)
    re, im = np.cos(phi), -np.sin(phi)
    mid = np.concatenate(
        [np.concatenate([re, -im], axis=2), np.concatenate([im, re], axis=2)], axis=1
    )
    back = np.swapaxes(mid, 1, 2)
    return [t.astype(ml_dtypes.bfloat16) for t in (first, mid, back, last)]


def spread_table(qblocks, copies, share):
    spread = np.einsum("ab,cd,e->acbed", np.eye(qblocks), np.eye(share), np.ones(copies))
    return spread.reshape(qblocks * share, -1).astype(ml_dtypes.bfloat16)


def dot(a, b):
    return jnp.dot(a, b, preferred_element_type=F32)


def turn(x, shift):
    width = x.shape[-1]
    shift %= width
    if width == 128:
        return pltpu.roll(x, shift, 1)
    return jnp.concatenate([x[:, width - shift :], x[:, : width - shift]], axis=1)


def lanes_of(shape):
    return lax.broadcasted_iota(jnp.int32, shape, len(shape) - 1)


def regroup(groups, count, unit, load, store, hold, steps):
    for place, step in enumerate(steps):
        for g in range(groups):
            for a in range(count):
                if a & step:
                    continue
                pair = [
                    load(g, k) if place == 0 else hold[g * count + k] for k in (a, a + step)
                ]
                lane = lanes_of(pair[0].shape)
                low = (lane // (unit * step)) % 2 == 0
                x = jnp.where(low, pair[0], turn(pair[1], unit * step))
                y = jnp.where(low, turn(pair[0], -unit * step), pair[1])
                if place == len(steps) - 1:
                    store(g, a, a + step, x, y)
                else:
                    hold[g * count + a] = x
                    hold[g * count + a + step] = y


def gather_lanes(xs, unit):
    return [
        jnp.concatenate([x[:, k * unit : (k + 1) * unit] for x in xs], axis=1)
        for k in range(xs[0].shape[1] // unit)
    ]


def prep_kernel(
    team, live_far, out_gate_far, key_far, value_far, cot_far, taps_far,
    out, key_out, value_out, cot, key, value, out_gate, taps, live, hold, hold_taps, sems,
):
    blocks, qlen, chans = key.shape
    lanes = out.shape[2]
    share = lanes // (2 * blocks)
    span = min(chans, 128)
    per = span // share
    spans = chans // span
    place = lax.rem(lax.axis_index("dp"), team)
    parts = 2
    size = qlen // parts
    taps_copy = pltpu.make_async_copy(taps_far.at[place], taps, sems.at[0])
    live_copy = pltpu.make_async_copy(live_far, live, sems.at[1])
    copies = []
    for part in range(parts):
        rows = pl.ds(part * size, size)
        copies.append([
            pltpu.make_async_copy(far.at[:, rows], near.at[:, rows], sems.at[2 + 4 * part + i])
            for i, (far, near) in enumerate(
                [(key_far, key), (value_far, value), (cot_far, cot), (out_gate_far, out_gate)]
            )
        ])
    live_copy.start()
    for copy in copies[0]:
        copy.start()
    taps_copy.start()
    for group in copies[1:]:
        for copy in group:
            copy.start()
    live_copy.wait()

    def load(g, a):
        part, m = g // spans, g % spans
        if a == 0 and m == 0:
            for copy in copies[part]:
                copy.wait()
        p = a % blocks
        rows = slice(part * size, (part + 1) * size)
        cols = slice(m * span, (m + 1) * span)
        if a >= blocks:
            wide = cot[p, rows, cols].astype(F32)
            return (wide * out_gate[p, rows, cols].astype(F32)).astype(BF16)
        alive = live[0, p].astype(F32)
        kept = key[p, rows, cols].astype(F32) * alive
        wide = value[p, rows, cols].astype(F32)
        key_out[p, rows, cols] = kept.astype(BF16)
        value_out[p, rows, cols] = (wide * alive).astype(BF16)
        return (kept * wide).astype(BF16)

    def store(g, a, b, x, y):
        part, m = g // spans, g % spans
        rows = slice(part * size, (part + 1) * size)
        out[m * per + a, rows, :] = x
        out[m * per + b, rows, :] = y

    def load_taps(g, a):
        return taps[a * SUB : (a + 1) * SUB, g * span : (g + 1) * span].astype(F32)

    def store_taps(g, a, b, x, y):
        out[g * per + a, qlen:, :] = x.astype(BF16)
        out[g * per + b, qlen:, :] = y.astype(BF16)

    if lanes == span:
        regroup(parts * spans, 2 * blocks, share, load, store, hold, (1, 2, 4))
        taps_copy.wait()
        regroup(spans, qlen // SUB, share, load_taps, store_taps, hold_taps, (1, 2, 4))
    else:
        taps_copy.wait()
        for g in range(parts * spans):
            xs = gather_lanes([load(g, a) for a in range(2 * blocks)], share)
            for k in range(0, per, 2):
                store(g, k, k + 1, xs[k], xs[k + 1])
        for g in range(spans):
            xs = gather_lanes([load_taps(g, a) for a in range(qlen // SUB)], share)
            for k in range(0, per, 2):
                store_taps(g, k, k + 1, xs[k], xs[k + 1])


def pair_tiles(a, b, qblocks):
    width = a.shape[1]
    ends = [x.reshape(qblocks, 1, SUB, width) for x in (a, b)]
    return jnp.concatenate(ends, axis=1).reshape(qblocks, 2 * SUB, width).astype(BF16)


def main_kernel(
    recv, first, spread, turns, last,
    out, signal_held, taps_held, rows_held, held, hold, pre, post, taps_out,
):
    full_rows, width = recv.shape[1:]
    prow = turns.shape[0] // 2
    qlen = turns.shape[1] // 2
    qblocks = qlen // SUB
    team = qblocks // 2
    groups = recv.shape[0] // team
    blocks = prow // groups
    each = blocks * SUB
    share = width // qblocks

    for i in range(groups):
        for p in range(0, blocks, 2):
            rows = slice(i * each + p * SUB, i * each + (p + 2) * SUB)
            ends = [recv[(p + e) * groups + i, qlen:, :].astype(F32) for e in (0, 1)]
            taps_held[rows, :] = jnp.concatenate(ends, axis=0).astype(BF16)

    def load(i, b):
        return recv[b * groups + i, :qlen, :]

    def store(i, a, b, x, y):
        rows = slice(i * each + a * SUB, i * each + (a + 2) * SUB)
        signal_held[:, rows, :width] = pair_tiles(x.astype(F32), y.astype(F32), qblocks)

    regroup(groups, blocks, share, load, store, hold, (2, 1))
    for qb in range(qblocks):
        table = spread[:, qb * width : (qb + 1) * width]
        signal_held[qb, :, width:] = dot(taps_held[...], table).astype(BF16)
    for qb in range(0, qblocks, 2):
        ends = [
            dot(first[...], signal_held[qb + e]).reshape(2 * prow, SUB, 2 * width) for e in (0, 1)
        ]
        rows_held[:, qb * SUB : (qb + 2) * SUB, :] = jnp.concatenate(ends, axis=1).astype(BF16)

    low = lanes_of((qlen, width)) < width // 2

    def step(m, carry):
        ends = []
        for e in (0, 1):
            k1 = 2 * m + e
            rows = rows_held[pl.ds(2 * k1, 2)].reshape(2 * qlen, 2 * width)
            full = dot(turns[k1], rows)
            re, im = full[:qlen, :width], full[qlen:, :width]
            hre, him = full[:qlen, width:], full[qlen:, width:]
            him = jnp.where(low, him, -him)
            ore, oim = turn(re, width // 2), turn(im, width // 2)
            tim = im * ore - re * oim
            real = jnp.concatenate([re * hre - im * him, re * ore + im * oim], axis=1)
            imag = jnp.concatenate([re * him + im * hre, jnp.where(low, -tim, tim)], axis=1)
            both = jnp.concatenate([real, imag], axis=0).astype(BF16)
            ends.append(dot(turns[prow + k1], both))
        parts = [x.reshape(2, qblocks, 1, SUB, 2 * width) for x in ends]
        both = jnp.concatenate(parts, axis=2).reshape(2, qblocks, 2 * SUB, 2 * width).astype(BF16)
        for qb in range(qblocks):
            for r in (0, 1):
                start = pl.multiple_of(m * 4 * SUB + r * 2 * SUB, 2 * SUB)
                held[qb, pl.ds(start, 2 * SUB), :] = both[r, qb]
        return carry

    lax.fori_loop(0, prow // 2, step, 0, unroll=8)

    for qb in range(0, qblocks, 2):
        ends = []
        for e in (0, 1):
            seq = dot(last[...], held[qb + e])
            ends.append(seq[:, :width].reshape(groups, blocks, SUB, width))
            taps_out[qb + e] = seq[:, width:]
        for p in range(blocks):
            both = jnp.concatenate([x[:, p] for x in ends], axis=1).astype(BF16)
            pre[qb // 2 * blocks + p] = both.reshape(groups * 2 * SUB, width)

    def load_out(g, a):
        return pre[g * blocks + a]

    def store_out(g, a, b, x, y):
        rows = slice(g * 2 * SUB, (g + 1) * 2 * SUB)
        out[a * groups : (a + 1) * groups, rows, :] = x.reshape(groups, 2 * SUB, width)
        out[b * groups : (b + 1) * groups, rows, :] = y.reshape(groups, 2 * SUB, width)

    regroup(qblocks // 2, blocks, share, load_out, store_out, post, (1, 2))
    lane = lanes_of((each, width)) // share
    for i in range(groups):
        rows = slice(i * each, (i + 1) * each)
        xs = [taps_out[qb, rows, :] for qb in range(qblocks)]
        step = 1
        while step < team:
            low = (lane // step) % 2 == 0
            xs = [
                jnp.where(low, x, y) + turn(jnp.where(low, y, x), step * share)
                for x, y in zip(xs[::2], xs[1::2])
            ]
            step *= 2
        while len(xs) > 1:
            low = (lane // step) % 2 == 0
            xs = [jnp.where(low, x, y) for x, y in zip(xs[::2], xs[1::2])]
            step *= 2
        halves = xs[0].reshape(blocks // 2, 2 * SUB, width).astype(BF16)
        for b in range(team):
            out[b * groups + i, qlen:, :] = halves[b % 2]


def post_kernel(
    recv, key, value, cot, gate_far, key_far, value_far, gate_out, key_out, value_out, hold, sems
):
    blocks, qlen, chans = key.shape
    width = recv.shape[2]
    share = width // (2 * blocks)
    span = min(chans, 128)
    per = span // share
    spans = chans // span
    parts = 2
    size = qlen // parts
    copies = []

    def load(g, a):
        part, m = g // spans, g % spans
        return recv[m * per + a, part * size : (part + 1) * size, :]

    def store_one(g, a, x):
        part, m = g // spans, g % spans
        rows = slice(part * size, (part + 1) * size)
        cols = slice(m * span, (m + 1) * span)
        x = x.astype(F32)
        if a < blocks:
            gate_out[a, rows, cols] = (cot[a, rows, cols].astype(F32) * x).astype(BF16)
        else:
            p = a - blocks
            key_out[p, rows, cols] = (x * value[p, rows, cols].astype(F32)).astype(BF16)
            value_out[p, rows, cols] = (x * key[p, rows, cols].astype(F32)).astype(BF16)

    def store(g, a, b, x, y):
        store_one(g, a, x)
        store_one(g, b, y)
        if g % spans == spans - 1 and b == 2 * blocks - 1:
            part = g // spans
            rows = pl.ds(part * size, size)
            for i, (near, far) in enumerate(
                [(gate_out, gate_far), (key_out, key_far), (value_out, value_far)]
            ):
                copy = pltpu.make_async_copy(
                    near.at[:, rows], far.at[:, rows], sems.at[3 * part + i]
                )
                copy.start()
                copies.append(copy)

    if width == span:
        regroup(parts * spans, per, share, load, store, hold, (1, 2, 4))
    else:
        for g in range(parts * spans):
            xs = gather_lanes([load(g, a) for a in range(per)], share)
            for a in range(0, 2 * blocks, 2):
                store(g, a, a + 1, xs[a], xs[a + 1])
    for copy in copies:
        copy.wait()


def finish_kernel(scale, mine, theirs, out, hold):
    blocks, qlen, chans = out.shape
    width = mine.shape[2]
    share = width // (qlen // SUB)
    span = min(chans, 128)
    per = span // share
    spans = chans // span
    flip = lax.rem(lax.axis_index("dp"), 2) == 0

    def load(g, a):
        c, m = g // spans, g % spans
        x, y = mine[m * per + a], theirs[m * per + a]
        return jnp.where(flip == (c == 0), x, y)

    def store(g, a, b, x, y):
        c, m = g // spans, g % spans
        ends = [z.astype(F32) * scale for z in (x, y)]
        for e in (0, 1):
            rows = slice(e * SUB, (e + 1) * SUB)
            both = jnp.concatenate([z[rows] for z in ends], axis=0).astype(BF16)
            out[2 * c + e, a * SUB : (a + 2) * SUB, m * span : (m + 1) * span] = both

    if width == span:
        regroup(2 * spans, per, share, load, store, hold, (4, 2, 1))
    else:
        for g in range(2 * spans):
            xs = gather_lanes([load(g, a) for a in range(per)], share)
            for a in range(0, qlen // SUB, 2):
                store(g, a, a + 1, xs[a], xs[a + 1])


VM = pl.BlockSpec(memory_space=pltpu.VMEM)
FAR = pl.BlockSpec(memory_space=pltpu.HBM)


def call(kernel, ins, outs, scratch=(), name=None, flops=0, out_specs=None, in_specs=None):
    nbytes = sum(math.prod(x.shape) * 2 for x in [*ins, *outs])
    held = nbytes + sum(math.prod(x.shape) * 2 for x in scratch if x.dtype == BF16)
    held += sum(math.prod(x.shape) * 4 for x in scratch if x.dtype == F32)
    return pl.pallas_call(
        kernel,
        out_shape=outs if len(outs) > 1 else outs[0],
        in_specs=in_specs or [VM] * len(ins),
        out_specs=out_specs or ([VM] * len(outs) if len(outs) > 1 else VM),
        scratch_shapes=list(scratch),
        compiler_params=pltpu.CompilerParams(vmem_limit_bytes=held + SPARE),
        cost_estimate=pl.CostEstimate(flops=flops, bytes_accessed=nbytes, transcendentals=0),
        name=name,
    )(*ins)


def shaped(shape, dtype=BF16):
    return jax.ShapeDtypeStruct(shape, dtype)


def local(out_gate, key_gate, value_input, filter_taps, cotangent, block_live):
    ctx = lax.axis_size("ctx")
    dp = lax.axis_size("dp")
    team = TEAM
    tok, chans = key_gate.shape[1:]
    blocks = block_live.shape[1]
    qlen = tok // blocks
    prow = blocks * ctx
    qblocks = qlen // SUB
    share = chans // (ctx * team)
    width = 2 * team * share
    peers = team * ctx
    grid = (blocks, qlen, chans)
    halves = (2 * blocks * chans // min(chans, 128) * 2, qlen // 2, min(chans, 128))
    first, mid, back, last = transform_tables(prow, qlen)
    first, last = jnp.asarray(first), jnp.asarray(last)
    turns = jnp.asarray(np.concatenate([mid, back]))
    spread = jnp.asarray(spread_table(qblocks, 2 * team, share))
    teams = None
    if dp > team:
        teams = [
            [(start + b) * ctx + i for b in range(team) for i in range(ctx)]
            for start in range(0, dp, team)
        ]

    def trade(x, bit):
        return lax.ppermute(x, "dp", [(i, i ^ bit) for i in range(dp)])

    def exchange(x):
        return lax.all_to_all(
            x, ("dp", "ctx"), split_axis=0, concat_axis=0, tiled=True, axis_index_groups=teams
        )

    packed, key, value, cot = call(
        functools.partial(prep_kernel, team),
        [
            pltpu.with_memory_space_constraint(x, pltpu.HBM)
            for x in (
                block_live,
                out_gate.reshape(grid),
                key_gate.reshape(grid),
                value_input.reshape(grid),
                cotangent.reshape(grid),
                filter_taps.reshape(grid),
            )
        ],
        [shaped((peers, qlen + SUB, width))] + [shaped(grid)] * 3,
        scratch=[
            *[pltpu.VMEM(grid, BF16)] * 3,
            pltpu.VMEM((qlen, chans), BF16),
            pltpu.SMEM(block_live.shape, jnp.int32),
            pltpu.VMEM(halves, BF16),
            pltpu.VMEM((peers, SUB, width), F32),
            pltpu.SemaphoreType.DMA((10,)),
        ],
        in_specs=[FAR] * 6,
        name="gate_and_pack",
        flops=10**10,
    )
    tables = [first, spread, turns, last]
    outs = call(
        main_kernel,
        [
            exchange(packed),
            *tables,
        ],
        [shaped((peers, qlen + 2 * SUB, width))],
        scratch=[
            pltpu.VMEM((qblocks, prow * SUB, 2 * width), BF16),
            pltpu.VMEM((prow * SUB, width), BF16),
            pltpu.VMEM((2 * prow, qlen, 2 * width), BF16),
            pltpu.VMEM((qblocks, 2 * prow * SUB, 2 * width), BF16),
            pltpu.VMEM((ctx * blocks, qlen, width), BF16),
            pltpu.VMEM((qblocks // 2 * blocks, ctx * 2 * SUB, width), BF16),
            pltpu.VMEM((qblocks // 2 * blocks, ctx * 2 * SUB, width), BF16),
            pltpu.VMEM((qblocks, prow * SUB, width), F32),
        ],
        name="convolve",
    )
    bit = team
    while bit < dp:
        part = outs[:, qlen:, :]
        total = part.astype(F32) + trade(part, bit).astype(F32)
        outs = lax.dynamic_update_slice(outs, total.astype(BF16), (0, qlen, 0))
        bit *= 2
    recv = exchange(outs)
    mine = recv[:, qlen:, :]
    theirs = trade(mine, 1)
    grads = call(
        post_kernel,
        [recv, key, value, cot],
        [shaped(grid)] * 3,
        scratch=[pltpu.VMEM(grid, BF16)] * 3
        + [pltpu.VMEM(halves, BF16), pltpu.SemaphoreType.DMA((6,))],
        out_specs=[FAR] * 3,
        name="ungate",
    )
    scale = 1.0 / math.sqrt(dp * tok * ctx)
    grad_taps = call(
        functools.partial(finish_kernel, scale),
        [mine, theirs],
        [shaped(grid)],
        scratch=[pltpu.VMEM((2 * peers, 2 * SUB, width), BF16)],
        name="scale_taps",
    )
    return (*[x.reshape(key_gate.shape) for x in grads], grad_taps.reshape(filter_taps.shape))


def solution(mesh):
    return jax.shard_map(
        local,
        mesh=mesh,
        in_specs=(
            P("dp", "ctx", None),
            P("dp", "ctx", None),
            P("dp", "ctx", None),
            P("ctx", None),
            P("dp", "ctx", None),
            P("dp", "ctx"),
        ),
        out_specs=(
            P("dp", "ctx", None),
            P("dp", "ctx", None),
            P("dp", "ctx", None),
            P("ctx", None),
        ),
        check_vma=False,
    )
```

```python
import functools
import itertools
import math
import random

import jax
import jax.numpy as jnp
import ml_dtypes
import numpy as np
from jax import lax
from jax.experimental import pallas as pl
from jax.experimental.pallas import tpu as pltpu
from jax.sharding import PartitionSpec as P


SUB = 8
TEAM = 4
SEED = 38
SPARE = 4 * 1024 * 1024
F32 = jnp.float32
BF16 = jnp.bfloat16


def transform_tables(prow, qlen):
    total = prow * qlen
    k1 = np.arange(prow)
    p = np.arange(prow)
    theta = 2.0 * np.pi * (((4 * k1[:, None] + 1) * p[None, :]) % (4 * prow)) / (4 * prow)
    eye = np.eye(SUB)
    first = np.stack([np.cos(theta), -np.sin(theta)], axis=1)
    first = np.einsum("krp,ab->krapb", first, eye).reshape(prow * 2 * SUB, prow * SUB)
    last = np.stack([np.cos(theta), -np.sin(theta)], axis=0) / total
    last = last.reshape(2, prow // 2, 2, prow)
    last = np.einsum("rmlp,ab->pamrlb", last, eye).reshape(prow * SUB, prow * 2 * SUB)
    q = np.arange(qlen)
    k2 = np.arange(qlen)
    phase = (4 * k1[:, None, None] + 1 + 4 * prow * k2[None, :, None]) * q[None, None, :]
    phi = 2.0 * np.pi * (phase % (4 * total)) / (4 * total)
    re, im = np.cos(phi), -np.sin(phi)
    mid = np.concatenate(
        [np.concatenate([re, -im], axis=2), np.concatenate([im, re], axis=2)], axis=1
    )
    back = np.swapaxes(mid, 1, 2)
    return [t.astype(ml_dtypes.bfloat16) for t in (first, mid, back, last)]


def spread_table(qblocks, copies, share):
    spread = np.einsum("ab,cd,e->acbed", np.eye(qblocks), np.eye(share), np.ones(copies))
    return spread.reshape(qblocks * share, -1).astype(ml_dtypes.bfloat16)


def dot(a, b):
    return jnp.dot(a, b, preferred_element_type=F32)


def turn(x, shift):
    width = x.shape[-1]
    shift %= width
    if width == 128:
        return pltpu.roll(x, shift, 1)
    return jnp.concatenate([x[:, width - shift :], x[:, : width - shift]], axis=1)


def lanes_of(shape):
    return lax.broadcasted_iota(jnp.int32, shape, len(shape) - 1)


def regroup(groups, count, unit, load, store, hold, steps):
    for place, step in enumerate(steps):
        for g in groups:
            for a in range(count):
                if a & step:
                    continue
                pair = [
                    load(g, k) if place == 0 else hold[g * count + k] for k in (a, a + step)
                ]
                lane = lanes_of(pair[0].shape)
                low = (lane // (unit * step)) % 2 == 0
                x = jnp.where(low, pair[0], turn(pair[1], unit * step))
                y = jnp.where(low, turn(pair[0], -unit * step), pair[1])
                if place == len(steps) - 1:
                    store(g, a, a + step, x, y)
                else:
                    hold[g * count + a] = x
                    hold[g * count + a + step] = y


def gather_lanes(xs, unit):
    return [
        jnp.concatenate([x[:, k * unit : (k + 1) * unit] for x in xs], axis=1)
        for k in range(xs[0].shape[1] // unit)
    ]


def prep_kernel(
    team, live_far, out_gate_far, key_far, value_far, cot_far, taps_far,
    out, key_out, value_out, cot, key, value, out_gate, taps, live, hold, hold_taps, sems,
):
    blocks, qlen, chans = key.shape
    lanes = out.shape[2]
    share = lanes // (2 * blocks)
    span = min(chans, 128)
    per = span // share
    spans = chans // span
    place = lax.rem(lax.axis_index("dp"), team)
    parts = 2
    size = qlen // parts
    taps_copy = pltpu.make_async_copy(taps_far.at[place], taps, sems.at[0])
    live_copy = pltpu.make_async_copy(live_far, live, sems.at[1])
    copies = []
    for part in range(parts):
        rows = pl.ds(part * size, size)
        copies.append([
            pltpu.make_async_copy(far.at[:, rows], near.at[:, rows], sems.at[2 + 4 * part + i])
            for i, (far, near) in enumerate(
                [(key_far, key), (value_far, value), (cot_far, cot), (out_gate_far, out_gate)]
            )
        ])
    taps_copy.start()
    live_copy.start()
    for group in copies:
        for copy in group:
            copy.start()

    def load(g, a):
        part, m = g // spans, g % spans
        p = a % blocks
        rows = slice(part * size, (part + 1) * size)
        cols = slice(m * span, (m + 1) * span)
        if a >= blocks:
            wide = cot[p, rows, cols].astype(F32)
            return (wide * out_gate[p, rows, cols].astype(F32)).astype(BF16)
        alive = live[0, p].astype(F32)
        kept = key[p, rows, cols].astype(F32) * alive
        wide = value[p, rows, cols].astype(F32)
        key_out[p, rows, cols] = kept.astype(BF16)
        value_out[p, rows, cols] = (wide * alive).astype(BF16)
        return (kept * wide).astype(BF16)

    def store(g, a, b, x, y):
        part, m = g // spans, g % spans
        rows = slice(part * size, (part + 1) * size)
        out[m * per + a, rows, :] = x
        out[m * per + b, rows, :] = y

    def load_taps(g, a):
        return taps[a * SUB : (a + 1) * SUB, g * span : (g + 1) * span].astype(F32)

    def store_taps(g, a, b, x, y):
        out[g * per + a, qlen:, :] = x.astype(BF16)
        out[g * per + b, qlen:, :] = y.astype(BF16)

    if lanes == span:
        taps_copy.wait()
        regroup(range(spans), qlen // SUB, share, load_taps, store_taps, hold_taps, (1, 2, 4))
        live_copy.wait()
        for part in range(parts):
            for copy in copies[part]:
                copy.wait()
            here = range(part * spans, (part + 1) * spans)
            regroup(here, 2 * blocks, share, load, store, hold, (1, 2, 4))
    else:
        for copy in [taps_copy, live_copy, *itertools.chain(*copies)]:
            copy.wait()
        for g in range(parts * spans):
            xs = gather_lanes([load(g, a) for a in range(2 * blocks)], share)
            for k in range(0, per, 2):
                store(g, k, k + 1, xs[k], xs[k + 1])
        for g in range(spans):
            xs = gather_lanes([load_taps(g, a) for a in range(qlen // SUB)], share)
            for k in range(0, per, 2):
                store_taps(g, k, k + 1, xs[k], xs[k + 1])


def pair_tiles(a, b, qblocks):
    width = a.shape[1]
    ends = [x.reshape(qblocks, 1, SUB, width) for x in (a, b)]
    return jnp.concatenate(ends, axis=1).reshape(qblocks, 2 * SUB, width).astype(BF16)


def main_kernel(
    seats, recv, first, spread, turns, last,
    out, signal_held, taps_held, rows_held, held, hold, pre, post, taps_out,
):
    full_rows, width = recv.shape[1:]
    prow = turns.shape[0] // 2
    qlen = turns.shape[1] // 2
    qblocks = qlen // SUB
    team = qblocks // 2
    groups = recv.shape[0] // team
    blocks = prow // groups
    each = blocks * SUB
    share = width // qblocks

    for i in range(groups):
        for p in range(0, blocks, 2):
            rows = slice(i * each + p * SUB, i * each + (p + 2) * SUB)
            ends = [recv[seats[p + e][i], qlen:, :].astype(F32) for e in (0, 1)]
            taps_held[rows, :] = jnp.concatenate(ends, axis=0).astype(BF16)

    def load(i, b):
        return recv[seats[b][i], :qlen, :]

    def store(i, a, b, x, y):
        rows = slice(i * each + a * SUB, i * each + (a + 2) * SUB)
        signal_held[:, rows, :width] = pair_tiles(x.astype(F32), y.astype(F32), qblocks)

    regroup(range(groups), blocks, share, load, store, hold, (2, 1))
    for qb in range(qblocks):
        table = spread[:, qb * width : (qb + 1) * width]
        signal_held[qb, :, width:] = dot(taps_held[...], table).astype(BF16)
    for qb in range(0, qblocks, 2):
        ends = [
            dot(first[...], signal_held[qb + e]).reshape(2 * prow, SUB, 2 * width) for e in (0, 1)
        ]
        rows_held[:, qb * SUB : (qb + 2) * SUB, :] = jnp.concatenate(ends, axis=1).astype(BF16)

    low = lanes_of((qlen, width)) < width // 2

    def step(m, carry):
        ends = []
        for e in (0, 1):
            k1 = 2 * m + e
            rows = rows_held[pl.ds(2 * k1, 2)].reshape(2 * qlen, 2 * width)
            full = dot(turns[k1], rows)
            re, im = full[:qlen, :width], full[qlen:, :width]
            hre, him = full[:qlen, width:], full[qlen:, width:]
            him = jnp.where(low, him, -him)
            ore, oim = turn(re, width // 2), turn(im, width // 2)
            tim = im * ore - re * oim
            real = jnp.concatenate([re * hre - im * him, re * ore + im * oim], axis=1)
            imag = jnp.concatenate([re * him + im * hre, jnp.where(low, -tim, tim)], axis=1)
            both = jnp.concatenate([real, imag], axis=0).astype(BF16)
            ends.append(dot(turns[prow + k1], both))
        parts = [x.reshape(2, qblocks, 1, SUB, 2 * width) for x in ends]
        both = jnp.concatenate(parts, axis=2).reshape(2, qblocks, 2 * SUB, 2 * width).astype(BF16)
        for qb in range(qblocks):
            for r in (0, 1):
                start = pl.multiple_of(m * 4 * SUB + r * 2 * SUB, 2 * SUB)
                held[qb, pl.ds(start, 2 * SUB), :] = both[r, qb]
        return carry

    lax.fori_loop(0, prow // 2, step, 0, unroll=16)

    for qb in range(0, qblocks, 2):
        ends = []
        for e in (0, 1):
            seq = dot(last[...], held[qb + e])
            ends.append(seq[:, :width].reshape(groups, blocks, SUB, width))
            taps_out[qb + e] = seq[:, width:]
        for p in range(blocks):
            both = jnp.concatenate([x[:, p] for x in ends], axis=1).astype(BF16)
            pre[qb // 2 * blocks + p] = both.reshape(groups * 2 * SUB, width)

    def load_out(g, a):
        return pre[g * blocks + a]

    def store_out(g, a, b, x, y):
        rows = slice(g * 2 * SUB, (g + 1) * 2 * SUB)
        for i in range(groups):
            tile = slice(i * 2 * SUB, (i + 1) * 2 * SUB)
            out[seats[a][i], rows, :] = x[tile]
            out[seats[b][i], rows, :] = y[tile]

    regroup(range(qblocks // 2), blocks, share, load_out, store_out, post, (1, 2))
    lane = lanes_of((each, width)) // share
    for i in range(groups):
        rows = slice(i * each, (i + 1) * each)
        xs = [taps_out[qb, rows, :] for qb in range(qblocks)]
        step = 1
        while step < team:
            low = (lane // step) % 2 == 0
            xs = [
                jnp.where(low, x, y) + turn(jnp.where(low, y, x), step * share)
                for x, y in zip(xs[::2], xs[1::2])
            ]
            step *= 2
        while len(xs) > 1:
            low = (lane // step) % 2 == 0
            xs = [jnp.where(low, x, y) for x, y in zip(xs[::2], xs[1::2])]
            step *= 2
        halves = xs[0].reshape(blocks // 2, 2 * SUB, width).astype(BF16)
        for b in range(team):
            out[seats[b][i], qlen:, :] = halves[b % 2]


def post_kernel(
    recv, key, value, cot, gate_far, key_far, value_far, gate_out, key_out, value_out, hold, sems
):
    blocks, qlen, chans = key.shape
    width = recv.shape[2]
    share = width // (2 * blocks)
    span = min(chans, 128)
    per = span // share
    spans = chans // span
    parts = 2
    size = qlen // parts
    copies = []

    def load(g, a):
        part, m = g // spans, g % spans
        return recv[m * per + a, part * size : (part + 1) * size, :]

    def store_one(g, a, x):
        part, m = g // spans, g % spans
        rows = slice(part * size, (part + 1) * size)
        cols = slice(m * span, (m + 1) * span)
        x = x.astype(F32)
        if a < blocks:
            gate_out[a, rows, cols] = (cot[a, rows, cols].astype(F32) * x).astype(BF16)
        else:
            p = a - blocks
            key_out[p, rows, cols] = (x * value[p, rows, cols].astype(F32)).astype(BF16)
            value_out[p, rows, cols] = (x * key[p, rows, cols].astype(F32)).astype(BF16)

    def store(g, a, b, x, y):
        store_one(g, a, x)
        store_one(g, b, y)
        if g % spans == spans - 1 and b == 2 * blocks - 1:
            part = g // spans
            rows = pl.ds(part * size, size)
            for i, (near, far) in enumerate(
                [(gate_out, gate_far), (key_out, key_far), (value_out, value_far)]
            ):
                copy = pltpu.make_async_copy(
                    near.at[:, rows], far.at[:, rows], sems.at[3 * part + i]
                )
                copy.start()
                copies.append(copy)

    if width == span:
        for part in range(parts):
            here = range(part * spans, (part + 1) * spans)
            regroup(here, per, share, load, store, hold, (1, 2, 4))
    else:
        for g in range(parts * spans):
            xs = gather_lanes([load(g, a) for a in range(per)], share)
            for a in range(0, 2 * blocks, 2):
                store(g, a, a + 1, xs[a], xs[a + 1])
    for copy in copies:
        copy.wait()


def finish_kernel(scale, mine, theirs, out, hold):
    blocks, qlen, chans = out.shape
    width = mine.shape[2]
    share = width // (qlen // SUB)
    span = min(chans, 128)
    per = span // share
    spans = chans // span
    flip = lax.rem(lax.axis_index("dp"), 2) == 0

    def load(g, a):
        c, m = g // spans, g % spans
        x, y = mine[m * per + a], theirs[m * per + a]
        return jnp.where(flip == (c == 0), x, y)

    def store(g, a, b, x, y):
        c, m = g // spans, g % spans
        ends = [z.astype(F32) * scale for z in (x, y)]
        for e in (0, 1):
            rows = slice(e * SUB, (e + 1) * SUB)
            both = jnp.concatenate([z[rows] for z in ends], axis=0).astype(BF16)
            out[2 * c + e, a * SUB : (a + 2) * SUB, m * span : (m + 1) * span] = both

    if width == span:
        regroup(range(2 * spans), per, share, load, store, hold, (4, 2, 1))
    else:
        for g in range(2 * spans):
            xs = gather_lanes([load(g, a) for a in range(per)], share)
            for a in range(0, qlen // SUB, 2):
                store(g, a, a + 1, xs[a], xs[a + 1])


VM = pl.BlockSpec(memory_space=pltpu.VMEM)
FAR = pl.BlockSpec(memory_space=pltpu.HBM)


def call(kernel, ins, outs, scratch=(), name=None, flops=0, out_specs=None, in_specs=None):
    nbytes = sum(math.prod(x.shape) * 2 for x in [*ins, *outs])
    held = nbytes + sum(math.prod(x.shape) * 2 for x in scratch if x.dtype == BF16)
    held += sum(math.prod(x.shape) * 4 for x in scratch if x.dtype == F32)
    return pl.pallas_call(
        kernel,
        out_shape=outs if len(outs) > 1 else outs[0],
        in_specs=in_specs or [VM] * len(ins),
        out_specs=out_specs or ([VM] * len(outs) if len(outs) > 1 else VM),
        scratch_shapes=list(scratch),
        compiler_params=pltpu.CompilerParams(vmem_limit_bytes=held + SPARE),
        cost_estimate=pl.CostEstimate(flops=flops, bytes_accessed=nbytes, transcendentals=0),
        name=name,
    )(*ins)


def shaped(shape, dtype=BF16):
    return jax.ShapeDtypeStruct(shape, dtype)


def local(out_gate, key_gate, value_input, filter_taps, cotangent, block_live):
    ctx = lax.axis_size("ctx")
    dp = lax.axis_size("dp")
    team = TEAM
    tok, chans = key_gate.shape[1:]
    blocks = block_live.shape[1]
    qlen = tok // blocks
    prow = blocks * ctx
    qblocks = qlen // SUB
    share = chans // (ctx * team)
    width = 2 * team * share
    peers = team * ctx
    grid = (blocks, qlen, chans)
    halves = (2 * blocks * chans // min(chans, 128) * 2, qlen // 2, min(chans, 128))
    first, mid, back, last = transform_tables(prow, qlen)
    first, last = jnp.asarray(first), jnp.asarray(last)
    turns = jnp.asarray(np.concatenate([mid, back]))
    spread = jnp.asarray(spread_table(qblocks, 2 * team, share))
    order = np.arange(peers)
    random.Random(SEED).shuffle(order)
    seats = np.argsort(order).reshape(team, ctx).tolist()
    teams = [(start * ctx + order).tolist() for start in range(0, dp, team)]

    def trade(x, bit):
        return lax.ppermute(x, "dp", [(i, i ^ bit) for i in range(dp)])

    def exchange(x):
        return lax.all_to_all(
            x, ("dp", "ctx"), split_axis=0, concat_axis=0, tiled=True, axis_index_groups=teams
        )

    packed, key, value, cot = call(
        functools.partial(prep_kernel, team),
        [
            pltpu.with_memory_space_constraint(x, pltpu.HBM)
            for x in (
                block_live,
                out_gate.reshape(grid),
                key_gate.reshape(grid),
                value_input.reshape(grid),
                cotangent.reshape(grid),
                filter_taps.reshape(grid),
            )
        ],
        [shaped((peers, qlen + SUB, width))] + [shaped(grid)] * 3,
        scratch=[
            *[pltpu.VMEM(grid, BF16)] * 3,
            pltpu.VMEM((qlen, chans), BF16),
            pltpu.SMEM(block_live.shape, jnp.int32),
            pltpu.VMEM(halves, BF16),
            pltpu.VMEM((peers, SUB, width), F32),
            pltpu.SemaphoreType.DMA((10,)),
        ],
        in_specs=[FAR] * 6,
        name="gate_and_pack",
        flops=10**10,
    )
    tables = [first, spread, turns, last]
    outs = call(
        functools.partial(main_kernel, seats),
        [
            exchange(packed),
            *tables,
        ],
        [shaped((peers, qlen + 2 * SUB, width))],
        scratch=[
            pltpu.VMEM((qblocks, prow * SUB, 2 * width), BF16),
            pltpu.VMEM((prow * SUB, width), BF16),
            pltpu.VMEM((2 * prow, qlen, 2 * width), BF16),
            pltpu.VMEM((qblocks, 2 * prow * SUB, 2 * width), BF16),
            pltpu.VMEM((ctx * blocks, qlen, width), BF16),
            pltpu.VMEM((qblocks // 2 * blocks, ctx * 2 * SUB, width), BF16),
            pltpu.VMEM((qblocks // 2 * blocks, ctx * 2 * SUB, width), BF16),
            pltpu.VMEM((qblocks, prow * SUB, width), F32),
        ],
        name="convolve",
    )
    bit = team
    while bit < dp:
        part = outs[:, qlen:, :]
        total = part.astype(F32) + trade(part, bit).astype(F32)
        outs = lax.dynamic_update_slice(outs, total.astype(BF16), (0, qlen, 0))
        bit *= 2
    recv = exchange(outs)
    mine = recv[:, qlen:, :]
    theirs = trade(mine, 1)
    grads = call(
        post_kernel,
        [recv, key, value, cot],
        [shaped(grid)] * 3,
        scratch=[pltpu.VMEM(grid, BF16)] * 3
        + [pltpu.VMEM(halves, BF16), pltpu.SemaphoreType.DMA((6,))],
        out_specs=[FAR] * 3,
        name="ungate",
    )
    scale = 1.0 / math.sqrt(dp * tok * ctx)
    grad_taps = call(
        functools.partial(finish_kernel, scale),
        [mine, theirs],
        [shaped(grid)],
        scratch=[pltpu.VMEM((2 * peers, 2 * SUB, width), BF16)],
        name="scale_taps",
    )
    return (*[x.reshape(key_gate.shape) for x in grads], grad_taps.reshape(filter_taps.shape))


def solution(mesh):
    return jax.shard_map(
        local,
        mesh=mesh,
        in_specs=(
            P("dp", "ctx", None),
            P("dp", "ctx", None),
            P("dp", "ctx", None),
            P("ctx", None),
            P("dp", "ctx", None),
            P("dp", "ctx"),
        ),
        out_specs=(
            P("dp", "ctx", None),
            P("dp", "ctx", None),
            P("dp", "ctx", None),
            P("ctx", None),
        ),
        check_vma=False,
    )
```

```python
import functools
import itertools
import math
import random

import jax
import jax.numpy as jnp
import ml_dtypes
import numpy as np
from jax import lax
from jax.experimental import pallas as pl
from jax.experimental.pallas import tpu as pltpu
from jax.sharding import PartitionSpec as P


SUB = 8
TEAM = 4
SEED = 38
SPARE = 4 * 1024 * 1024
F32 = jnp.float32
BF16 = jnp.bfloat16


def transform_tables(prow, qlen):
    total = prow * qlen
    k1 = np.arange(prow)
    p = np.arange(prow)
    theta = 2.0 * np.pi * (((4 * k1[:, None] + 1) * p[None, :]) % (4 * prow)) / (4 * prow)
    eye = np.eye(SUB)
    first = np.stack([np.cos(theta), -np.sin(theta)], axis=1)
    first = np.einsum("krp,ab->krapb", first, eye).reshape(prow * 2 * SUB, prow * SUB)
    last = np.stack([np.cos(theta), -np.sin(theta)], axis=0) / total
    last = last.reshape(2, prow // 2, 2, prow)
    last = np.einsum("rmlp,ab->pamrlb", last, eye).reshape(prow * SUB, prow * 2 * SUB)
    q = np.arange(qlen)
    k2 = np.arange(qlen)
    phase = (4 * k1[:, None, None] + 1 + 4 * prow * k2[None, :, None]) * q[None, None, :]
    phi = 2.0 * np.pi * (phase % (4 * total)) / (4 * total)
    re, im = np.cos(phi), -np.sin(phi)
    mid = np.concatenate(
        [np.concatenate([re, -im], axis=2), np.concatenate([im, re], axis=2)], axis=1
    )
    back = np.swapaxes(mid, 1, 2)
    return [t.astype(ml_dtypes.bfloat16) for t in (first, mid, back, last)]


def spread_table(qblocks, copies, share):
    spread = np.einsum("ab,cd,e->acbed", np.eye(qblocks), np.eye(share), np.ones(copies))
    return spread.reshape(qblocks * share, -1).astype(ml_dtypes.bfloat16)


def dot(a, b):
    return jnp.dot(a, b, preferred_element_type=F32)


def turn(x, shift):
    width = x.shape[-1]
    shift %= width
    if width == 128:
        return pltpu.roll(x, shift, 1)
    return jnp.concatenate([x[:, width - shift :], x[:, : width - shift]], axis=1)


def lanes_of(shape):
    return lax.broadcasted_iota(jnp.int32, shape, len(shape) - 1)


def regroup(groups, count, unit, load, store, hold, steps):
    for place, step in enumerate(steps):
        for g in groups:
            for a in range(count):
                if a & step:
                    continue
                pair = [
                    load(g, k) if place == 0 else hold[g * count + k] for k in (a, a + step)
                ]
                lane = lanes_of(pair[0].shape)
                low = (lane // (unit * step)) % 2 == 0
                x = jnp.where(low, pair[0], turn(pair[1], unit * step))
                y = jnp.where(low, turn(pair[0], -unit * step), pair[1])
                if place == len(steps) - 1:
                    store(g, a, a + step, x, y)
                else:
                    hold[g * count + a] = x
                    hold[g * count + a + step] = y


def gather_lanes(xs, unit):
    return [
        jnp.concatenate([x[:, k * unit : (k + 1) * unit] for x in xs], axis=1)
        for k in range(xs[0].shape[1] // unit)
    ]


def prep_kernel(
    team, live_far, out_gate_far, key_far, value_far, cot_far, taps_far,
    out, key_out, value_out, cot, key, value, out_gate, taps, live, hold, hold_taps, sems,
):
    blocks, qlen, chans = key.shape
    lanes = out.shape[2]
    share = lanes // (2 * blocks)
    span = min(chans, 128)
    per = span // share
    spans = chans // span
    place = lax.rem(lax.axis_index("dp"), team)
    parts = 2
    size = qlen // parts
    taps_copy = pltpu.make_async_copy(taps_far.at[place], taps, sems.at[0])
    live_copy = pltpu.make_async_copy(live_far, live, sems.at[1])
    copies = []
    for part in range(parts):
        rows = pl.ds(part * size, size)
        copies.append([
            pltpu.make_async_copy(far.at[:, rows], near.at[:, rows], sems.at[2 + 4 * part + i])
            for i, (far, near) in enumerate(
                [(key_far, key), (value_far, value), (cot_far, cot), (out_gate_far, out_gate)]
            )
        ])
    taps_copy.start()
    live_copy.start()
    for group in copies:
        for copy in group:
            copy.start()

    def load(g, a):
        part, m = g // spans, g % spans
        if lanes == span and a == 0 and m == 0:
            for copy in copies[part]:
                copy.wait()
        p = a % blocks
        rows = slice(part * size, (part + 1) * size)
        cols = slice(m * span, (m + 1) * span)
        if a >= blocks:
            return cot[p, rows, cols] * out_gate[p, rows, cols]
        dead = live[0, p] == 0
        none = jnp.zeros((size, span), BF16)
        kept = jnp.where(dead, none, key[p, rows, cols])
        kept_value = jnp.where(dead, none, value[p, rows, cols])
        key_out[p, rows, cols] = kept
        value_out[p, rows, cols] = kept_value
        return kept * kept_value

    def store(g, a, b, x, y):
        part, m = g // spans, g % spans
        rows = slice(part * size, (part + 1) * size)
        out[m * per + a, rows, :] = x
        out[m * per + b, rows, :] = y

    def load_taps(g, a):
        return taps[a * SUB : (a + 1) * SUB, g * span : (g + 1) * span].astype(F32)

    def store_taps(g, a, b, x, y):
        out[g * per + a, qlen:, :] = x.astype(BF16)
        out[g * per + b, qlen:, :] = y.astype(BF16)

    if lanes == span:
        taps_copy.wait()
        regroup(range(spans), qlen // SUB, share, load_taps, store_taps, hold_taps, (1, 2, 4))
        live_copy.wait()
        regroup(range(parts * spans), 2 * blocks, share, load, store, hold, (1, 2, 4))
    else:
        for copy in [taps_copy, live_copy, *itertools.chain(*copies)]:
            copy.wait()
        for g in range(parts * spans):
            xs = gather_lanes([load(g, a) for a in range(2 * blocks)], share)
            for k in range(0, per, 2):
                store(g, k, k + 1, xs[k], xs[k + 1])
        for g in range(spans):
            xs = gather_lanes([load_taps(g, a) for a in range(qlen // SUB)], share)
            for k in range(0, per, 2):
                store_taps(g, k, k + 1, xs[k], xs[k + 1])


def pair_tiles(a, b, qblocks):
    width = a.shape[1]
    ends = [x.reshape(qblocks, 1, SUB, width) for x in (a, b)]
    return jnp.concatenate(ends, axis=1).reshape(qblocks, 2 * SUB, width).astype(BF16)


def main_kernel(
    seats, recv, first, spread, turns, last,
    out, signal_held, taps_held, rows_held, held, hold, pre, post, taps_out,
):
    full_rows, width = recv.shape[1:]
    prow = turns.shape[0] // 2
    qlen = turns.shape[1] // 2
    qblocks = qlen // SUB
    team = qblocks // 2
    groups = recv.shape[0] // team
    blocks = prow // groups
    each = blocks * SUB
    share = width // qblocks

    for i in range(groups):
        for p in range(0, blocks, 2):
            rows = slice(i * each + p * SUB, i * each + (p + 2) * SUB)
            ends = [recv[seats[p + e][i], qlen:, :].astype(F32) for e in (0, 1)]
            taps_held[rows, :] = jnp.concatenate(ends, axis=0).astype(BF16)

    def load(i, b):
        return recv[seats[b][i], :qlen, :]

    def store(i, a, b, x, y):
        rows = slice(i * each + a * SUB, i * each + (a + 2) * SUB)
        signal_held[:, rows, :width] = pair_tiles(x.astype(F32), y.astype(F32), qblocks)

    regroup(range(groups), blocks, share, load, store, hold, (2, 1))
    for qb in range(qblocks):
        table = spread[:, qb * width : (qb + 1) * width]
        signal_held[qb, :, width:] = dot(taps_held[...], table).astype(BF16)
    for qb in range(0, qblocks, 2):
        ends = [
            dot(first[...], signal_held[qb + e]).reshape(2 * prow, SUB, 2 * width) for e in (0, 1)
        ]
        rows_held[:, qb * SUB : (qb + 2) * SUB, :] = jnp.concatenate(ends, axis=1).astype(BF16)

    low = lanes_of((qlen, width)) < width // 2

    def step(m, carry):
        ends = []
        for e in (0, 1):
            k1 = 2 * m + e
            rows = rows_held[pl.ds(2 * k1, 2)].reshape(2 * qlen, 2 * width)
            full = dot(turns[k1], rows)
            re, im = full[:qlen, :width], full[qlen:, :width]
            hre, him = full[:qlen, width:], full[qlen:, width:]
            him = jnp.where(low, him, -him)
            ore, oim = turn(re, width // 2), turn(im, width // 2)
            tim = im * ore - re * oim
            real = jnp.concatenate([re * hre - im * him, re * ore + im * oim], axis=1)
            imag = jnp.concatenate([re * him + im * hre, jnp.where(low, -tim, tim)], axis=1)
            both = jnp.concatenate([real, imag], axis=0).astype(BF16)
            ends.append(dot(turns[prow + k1], both))
        parts = [x.reshape(2, qblocks, 1, SUB, 2 * width) for x in ends]
        both = jnp.concatenate(parts, axis=2).reshape(2, qblocks, 2 * SUB, 2 * width).astype(BF16)
        for qb in range(qblocks):
            for r in (0, 1):
                start = pl.multiple_of(m * 4 * SUB + r * 2 * SUB, 2 * SUB)
                held[qb, pl.ds(start, 2 * SUB), :] = both[r, qb]
        return carry

    lax.fori_loop(0, prow // 2, step, 0, unroll=16)

    for qb in range(0, qblocks, 2):
        ends = []
        for e in (0, 1):
            seq = dot(last[...], held[qb + e])
            ends.append(seq[:, :width].reshape(groups, blocks, SUB, width))
            taps_out[qb + e] = seq[:, width:]
        for p in range(blocks):
            both = jnp.concatenate([x[:, p] for x in ends], axis=1).astype(BF16)
            pre[qb // 2 * blocks + p] = both.reshape(groups * 2 * SUB, width)

    def load_out(g, a):
        return pre[g * blocks + a]

    def store_out(g, a, b, x, y):
        rows = slice(g * 2 * SUB, (g + 1) * 2 * SUB)
        for i in range(groups):
            tile = slice(i * 2 * SUB, (i + 1) * 2 * SUB)
            out[seats[a][i], rows, :] = x[tile]
            out[seats[b][i], rows, :] = y[tile]

    regroup(range(qblocks // 2), blocks, share, load_out, store_out, post, (1, 2))
    lane = lanes_of((each, width)) // share
    for i in range(groups):
        rows = slice(i * each, (i + 1) * each)
        xs = [taps_out[qb, rows, :] for qb in range(qblocks)]
        step = 1
        while step < team:
            low = (lane // step) % 2 == 0
            xs = [
                jnp.where(low, x, y) + turn(jnp.where(low, y, x), step * share)
                for x, y in zip(xs[::2], xs[1::2])
            ]
            step *= 2
        while len(xs) > 1:
            low = (lane // step) % 2 == 0
            xs = [jnp.where(low, x, y) for x, y in zip(xs[::2], xs[1::2])]
            step *= 2
        halves = xs[0].reshape(blocks // 2, 2 * SUB, width).astype(BF16)
        for b in range(team):
            out[seats[b][i], qlen:, :] = halves[b % 2]


def post_kernel(
    recv, key, value, cot, gate_far, key_far, value_far, gate_out, key_out, value_out, hold, sems
):
    blocks, qlen, chans = key.shape
    width = recv.shape[2]
    share = width // (2 * blocks)
    span = min(chans, 128)
    per = span // share
    spans = chans // span
    parts = 2
    size = qlen // parts
    copies = []

    def load(g, a):
        part, m = g // spans, g % spans
        return recv[m * per + a, part * size : (part + 1) * size, :]

    def store_one(g, a, x):
        part, m = g // spans, g % spans
        rows = slice(part * size, (part + 1) * size)
        cols = slice(m * span, (m + 1) * span)
        if a < blocks:
            gate_out[a, rows, cols] = cot[a, rows, cols] * x
        else:
            p = a - blocks
            key_out[p, rows, cols] = x * value[p, rows, cols]
            value_out[p, rows, cols] = x * key[p, rows, cols]

    def store(g, a, b, x, y):
        store_one(g, a, x)
        store_one(g, b, y)
        if g % spans == spans - 1 and b == 2 * blocks - 1:
            part = g // spans
            rows = pl.ds(part * size, size)
            for i, (near, far) in enumerate(
                [(gate_out, gate_far), (key_out, key_far), (value_out, value_far)]
            ):
                copy = pltpu.make_async_copy(
                    near.at[:, rows], far.at[:, rows], sems.at[3 * part + i]
                )
                copy.start()
                copies.append(copy)

    if width == span:
        regroup(range(parts * spans), per, share, load, store, hold, (1, 2, 4))
    else:
        for g in range(parts * spans):
            xs = gather_lanes([load(g, a) for a in range(per)], share)
            for a in range(0, 2 * blocks, 2):
                store(g, a, a + 1, xs[a], xs[a + 1])
    for copy in copies:
        copy.wait()


def finish_kernel(scale, mine, theirs, out, hold):
    blocks, qlen, chans = out.shape
    width = mine.shape[2]
    share = width // (qlen // SUB)
    span = min(chans, 128)
    per = span // share
    spans = chans // span
    flip = lax.rem(lax.axis_index("dp"), 2) == 0

    def load(g, a):
        c, m = g // spans, g % spans
        x, y = mine[m * per + a], theirs[m * per + a]
        return jnp.where(flip == (c == 0), x, y)

    def store(g, a, b, x, y):
        c, m = g // spans, g % spans
        ends = [z.astype(F32) * scale for z in (x, y)]
        for e in (0, 1):
            rows = slice(e * SUB, (e + 1) * SUB)
            both = jnp.concatenate([z[rows] for z in ends], axis=0).astype(BF16)
            out[2 * c + e, a * SUB : (a + 2) * SUB, m * span : (m + 1) * span] = both

    if width == span:
        regroup(range(2 * spans), per, share, load, store, hold, (4, 2, 1))
    else:
        for g in range(2 * spans):
            xs = gather_lanes([load(g, a) for a in range(per)], share)
            for a in range(0, qlen // SUB, 2):
                store(g, a, a + 1, xs[a], xs[a + 1])


VM = pl.BlockSpec(memory_space=pltpu.VMEM)
FAR = pl.BlockSpec(memory_space=pltpu.HBM)


def call(kernel, ins, outs, scratch=(), name=None, flops=0, out_specs=None, in_specs=None):
    nbytes = sum(math.prod(x.shape) * 2 for x in [*ins, *outs])
    held = nbytes + sum(math.prod(x.shape) * 2 for x in scratch if x.dtype == BF16)
    held += sum(math.prod(x.shape) * 4 for x in scratch if x.dtype == F32)
    return pl.pallas_call(
        kernel,
        out_shape=outs if len(outs) > 1 else outs[0],
        in_specs=in_specs or [VM] * len(ins),
        out_specs=out_specs or ([VM] * len(outs) if len(outs) > 1 else VM),
        scratch_shapes=list(scratch),
        compiler_params=pltpu.CompilerParams(vmem_limit_bytes=held + SPARE),
        cost_estimate=pl.CostEstimate(flops=flops, bytes_accessed=nbytes, transcendentals=0),
        name=name,
    )(*ins)


def shaped(shape, dtype=BF16):
    return jax.ShapeDtypeStruct(shape, dtype)


def local(out_gate, key_gate, value_input, filter_taps, cotangent, block_live):
    ctx = lax.axis_size("ctx")
    dp = lax.axis_size("dp")
    team = TEAM
    tok, chans = key_gate.shape[1:]
    blocks = block_live.shape[1]
    qlen = tok // blocks
    prow = blocks * ctx
    qblocks = qlen // SUB
    share = chans // (ctx * team)
    width = 2 * team * share
    peers = team * ctx
    grid = (blocks, qlen, chans)
    halves = (2 * blocks * chans // min(chans, 128) * 2, qlen // 2, min(chans, 128))
    first, mid, back, last = transform_tables(prow, qlen)
    first, last = jnp.asarray(first), jnp.asarray(last)
    turns = jnp.asarray(np.concatenate([mid, back]))
    spread = jnp.asarray(spread_table(qblocks, 2 * team, share))
    order = np.arange(peers)
    random.Random(SEED).shuffle(order)
    seats = np.argsort(order).reshape(team, ctx).tolist()
    teams = [(start * ctx + order).tolist() for start in range(0, dp, team)]

    def trade(x, bit):
        return lax.ppermute(x, "dp", [(i, i ^ bit) for i in range(dp)])

    def exchange(x):
        return lax.all_to_all(
            x, ("dp", "ctx"), split_axis=0, concat_axis=0, tiled=True, axis_index_groups=teams
        )

    packed, key, value, cot = call(
        functools.partial(prep_kernel, team),
        [
            pltpu.with_memory_space_constraint(x, pltpu.HBM)
            for x in (
                block_live,
                out_gate.reshape(grid),
                key_gate.reshape(grid),
                value_input.reshape(grid),
                cotangent.reshape(grid),
                filter_taps.reshape(grid),
            )
        ],
        [shaped((peers, qlen + SUB, width))] + [shaped(grid)] * 3,
        scratch=[
            *[pltpu.VMEM(grid, BF16)] * 3,
            pltpu.VMEM((qlen, chans), BF16),
            pltpu.SMEM(block_live.shape, jnp.int32),
            pltpu.VMEM(halves, BF16),
            pltpu.VMEM((peers, SUB, width), F32),
            pltpu.SemaphoreType.DMA((10,)),
        ],
        in_specs=[FAR] * 6,
        name="gate_and_pack",
        flops=10**10,
    )
    tables = [first, spread, turns, last]
    outs = call(
        functools.partial(main_kernel, seats),
        [
            exchange(packed),
            *tables,
        ],
        [shaped((peers, qlen + 2 * SUB, width))],
        scratch=[
            pltpu.VMEM((qblocks, prow * SUB, 2 * width), BF16),
            pltpu.VMEM((prow * SUB, width), BF16),
            pltpu.VMEM((2 * prow, qlen, 2 * width), BF16),
            pltpu.VMEM((qblocks, 2 * prow * SUB, 2 * width), BF16),
            pltpu.VMEM((ctx * blocks, qlen, width), BF16),
            pltpu.VMEM((qblocks // 2 * blocks, ctx * 2 * SUB, width), BF16),
            pltpu.VMEM((qblocks // 2 * blocks, ctx * 2 * SUB, width), BF16),
            pltpu.VMEM((qblocks, prow * SUB, width), F32),
        ],
        name="convolve",
    )
    bit = team
    while bit < dp:
        part = outs[:, qlen:, :]
        total = part.astype(F32) + trade(part, bit).astype(F32)
        outs = lax.dynamic_update_slice(outs, total.astype(BF16), (0, qlen, 0))
        bit *= 2
    recv = exchange(outs)
    mine = recv[:, qlen:, :]
    theirs = trade(mine, 1)
    grads = call(
        post_kernel,
        [recv, key, value, cot],
        [shaped(grid)] * 3,
        scratch=[pltpu.VMEM(grid, BF16)] * 3
        + [pltpu.VMEM(halves, BF16), pltpu.SemaphoreType.DMA((6,))],
        out_specs=[FAR] * 3,
        name="ungate",
    )
    scale = 1.0 / math.sqrt(dp * tok * ctx)
    grad_taps = call(
        functools.partial(finish_kernel, scale),
        [mine, theirs],
        [shaped(grid)],
        scratch=[pltpu.VMEM((2 * peers, 2 * SUB, width), BF16)],
        name="scale_taps",
    )
    return (*[x.reshape(key_gate.shape) for x in grads], grad_taps.reshape(filter_taps.shape))


def solution(mesh):
    return jax.shard_map(
        local,
        mesh=mesh,
        in_specs=(
            P("dp", "ctx", None),
            P("dp", "ctx", None),
            P("dp", "ctx", None),
            P("ctx", None),
            P("dp", "ctx", None),
            P("dp", "ctx"),
        ),
        out_specs=(
            P("dp", "ctx", None),
            P("dp", "ctx", None),
            P("dp", "ctx", None),
            P("ctx", None),
        ),
        check_vma=False,
    )
```

```python
import functools
import itertools
import math
import random

import jax
import jax.numpy as jnp
import ml_dtypes
import numpy as np
from jax import lax
from jax.experimental import pallas as pl
from jax.experimental.pallas import tpu as pltpu
from jax.sharding import PartitionSpec as P


SUB = 8
TEAM = 4
SEED = 38
SPARE = 4 * 1024 * 1024
F32 = jnp.float32
BF16 = jnp.bfloat16


def transform_tables(prow, qlen):
    total = prow * qlen
    k1 = np.arange(prow)
    p = np.arange(prow)
    theta = 2.0 * np.pi * (((4 * k1[:, None] + 1) * p[None, :]) % (4 * prow)) / (4 * prow)
    eye = np.eye(SUB)
    first = np.stack([np.cos(theta), -np.sin(theta)], axis=1)
    first = np.einsum("krp,ab->krapb", first, eye).reshape(prow * 2 * SUB, prow * SUB)
    last = np.stack([np.cos(theta), -np.sin(theta)], axis=0) / total
    last = last.reshape(2, prow // 2, 2, prow)
    last = np.einsum("rmlp,ab->pamrlb", last, eye).reshape(prow * SUB, prow * 2 * SUB)
    q = np.arange(qlen)
    k2 = np.arange(qlen)
    phase = (4 * k1[:, None, None] + 1 + 4 * prow * k2[None, :, None]) * q[None, None, :]
    phi = 2.0 * np.pi * (phase % (4 * total)) / (4 * total)
    re, im = np.cos(phi), -np.sin(phi)
    mid = np.concatenate(
        [np.concatenate([re, -im], axis=2), np.concatenate([im, re], axis=2)], axis=1
    )
    back = np.swapaxes(mid, 1, 2)
    return [t.astype(ml_dtypes.bfloat16) for t in (first, mid, back, last)]


def spread_table(qblocks, copies, share):
    spread = np.einsum("ab,cd,e->acbed", np.eye(qblocks), np.eye(share), np.ones(copies))
    return spread.reshape(qblocks * share, -1).astype(ml_dtypes.bfloat16)


def dot(a, b):
    return jnp.dot(a, b, preferred_element_type=F32)


def turn(x, shift):
    width = x.shape[-1]
    shift %= width
    if width == 128:
        return pltpu.roll(x, shift, 1)
    return jnp.concatenate([x[:, width - shift :], x[:, : width - shift]], axis=1)


def lanes_of(shape):
    return lax.broadcasted_iota(jnp.int32, shape, len(shape) - 1)


def skew(x, a, unit):
    return turn(x, unit * a) if a else x


def regroup(groups, count, unit, load, store, hold):
    if load is not None:
        for g in groups:
            for a in range(count):
                hold[g * count + a] = skew(load(g, a), a, unit)
    for g in groups:
        xs = [hold[g * count + (-k) % count] for k in range(count)]
        block = lanes_of(xs[0].shape) // unit
        step = 1
        while step < count:
            moved = (block // step) % 2 == 1
            xs = [jnp.where(moved, xs[b - step], xs[b]) for b in range(count)]
            step *= 2
        xs = [skew(x, -b, unit) for b, x in enumerate(xs)]
        for b in range(0, count, 2):
            store(g, b, b + 1, xs[b], xs[b + 1])


def gather_lanes(xs, unit):
    return [
        jnp.concatenate([x[:, k * unit : (k + 1) * unit] for x in xs], axis=1)
        for k in range(xs[0].shape[1] // unit)
    ]


def prep_kernel(
    team, live_far, out_gate_far, key_far, value_far, cot_far, taps_far,
    out, key_out, value_out, cot, key, value, out_gate, taps, live, hold, hold_taps, sems,
):
    blocks, qlen, chans = key.shape
    lanes = out.shape[2]
    share = lanes // (2 * blocks)
    span = min(chans, 128)
    per = span // share
    spans = chans // span
    place = lax.rem(lax.axis_index("dp"), team)
    parts = 2
    size = qlen // parts
    taps_copy = pltpu.make_async_copy(taps_far.at[place], taps, sems.at[0])
    live_copy = pltpu.make_async_copy(live_far, live, sems.at[1])
    copies = []
    for part in range(parts):
        rows = pl.ds(part * size, size)
        copies.append([
            pltpu.make_async_copy(far.at[:, rows], near.at[:, rows], sems.at[2 + 4 * part + i])
            for i, (far, near) in enumerate(
                [(key_far, key), (value_far, value), (cot_far, cot), (out_gate_far, out_gate)]
            )
        ])
    taps_copy.start()
    live_copy.start()
    for group in copies:
        for copy in group:
            copy.start()

    def load(g, a):
        part, m = g // spans, g % spans
        if lanes == span and a == 0 and m == 0:
            for copy in copies[part]:
                copy.wait()
        p = a % blocks
        rows = slice(part * size, (part + 1) * size)
        cols = slice(m * span, (m + 1) * span)
        if a >= blocks:
            return cot[p, rows, cols] * out_gate[p, rows, cols]
        dead = live[0, p] == 0
        none = jnp.zeros((size, span), BF16)
        kept = jnp.where(dead, none, key[p, rows, cols])
        kept_value = jnp.where(dead, none, value[p, rows, cols])
        key_out[p, rows, cols] = kept
        value_out[p, rows, cols] = kept_value
        return kept * kept_value

    def store(g, a, b, x, y):
        part, m = g // spans, g % spans
        rows = slice(part * size, (part + 1) * size)
        out[m * per + a, rows, :] = x
        out[m * per + b, rows, :] = y

    def load_taps(g, a):
        return taps[a * SUB : (a + 1) * SUB, g * span : (g + 1) * span].astype(F32)

    def store_taps(g, a, b, x, y):
        out[g * per + a, qlen:, :] = x.astype(BF16)
        out[g * per + b, qlen:, :] = y.astype(BF16)

    if lanes == span:
        taps_copy.wait()
        regroup(range(spans), qlen // SUB, share, load_taps, store_taps, hold_taps)
        live_copy.wait()
        regroup(range(parts * spans), 2 * blocks, share, load, store, hold)
    else:
        for copy in [taps_copy, live_copy, *itertools.chain(*copies)]:
            copy.wait()
        for g in range(parts * spans):
            xs = gather_lanes([load(g, a) for a in range(2 * blocks)], share)
            for k in range(0, per, 2):
                store(g, k, k + 1, xs[k], xs[k + 1])
        for g in range(spans):
            xs = gather_lanes([load_taps(g, a) for a in range(qlen // SUB)], share)
            for k in range(0, per, 2):
                store_taps(g, k, k + 1, xs[k], xs[k + 1])


def pair_tiles(a, b, qblocks):
    width = a.shape[1]
    ends = [x.reshape(qblocks, 1, SUB, width) for x in (a, b)]
    return jnp.concatenate(ends, axis=1).reshape(qblocks, 2 * SUB, width).astype(BF16)


def main_kernel(
    seats, recv, first, spread, turns, last,
    out, signal_held, taps_held, rows_held, held, hold, post, taps_out,
):
    full_rows, width = recv.shape[1:]
    prow = turns.shape[0] // 2
    qlen = turns.shape[1] // 2
    qblocks = qlen // SUB
    team = qblocks // 2
    groups = recv.shape[0] // team
    blocks = prow // groups
    each = blocks * SUB
    share = width // qblocks

    for i in range(groups):
        for p in range(0, blocks, 2):
            rows = slice(i * each + p * SUB, i * each + (p + 2) * SUB)
            ends = [recv[seats[p + e][i], qlen:, :].astype(F32) for e in (0, 1)]
            taps_held[rows, :] = jnp.concatenate(ends, axis=0).astype(BF16)

    def load(i, b):
        return recv[seats[b][i], :qlen, :]

    def store(i, a, b, x, y):
        rows = slice(i * each + a * SUB, i * each + (a + 2) * SUB)
        signal_held[:, rows, :width] = pair_tiles(x.astype(F32), y.astype(F32), qblocks)

    regroup(range(groups), blocks, share, load, store, hold)
    for qb in range(qblocks):
        table = spread[:, qb * width : (qb + 1) * width]
        signal_held[qb, :, width:] = dot(taps_held[...], table).astype(BF16)
    for qb in range(0, qblocks, 2):
        ends = [
            dot(first[...], signal_held[qb + e]).reshape(2 * prow, SUB, 2 * width) for e in (0, 1)
        ]
        rows_held[:, qb * SUB : (qb + 2) * SUB, :] = jnp.concatenate(ends, axis=1).astype(BF16)

    low = lanes_of((qlen, width)) < width // 2

    def step(m, carry):
        ends = []
        for e in (0, 1):
            k1 = 2 * m + e
            rows = rows_held[pl.ds(2 * k1, 2)].reshape(2 * qlen, 2 * width)
            full = dot(turns[k1], rows)
            re, im = full[:qlen, :width], full[qlen:, :width]
            hre, him = full[:qlen, width:], full[qlen:, width:]
            him = jnp.where(low, him, -him)
            ore, oim = turn(re, width // 2), turn(im, width // 2)
            tim = im * ore - re * oim
            real = jnp.concatenate([re * hre - im * him, re * ore + im * oim], axis=1)
            imag = jnp.concatenate([re * him + im * hre, jnp.where(low, -tim, tim)], axis=1)
            both = jnp.concatenate([real, imag], axis=0).astype(BF16)
            ends.append(dot(turns[prow + k1], both))
        parts = [x.reshape(2, qblocks, 1, SUB, 2 * width) for x in ends]
        both = jnp.concatenate(parts, axis=2).reshape(2, qblocks, 2 * SUB, 2 * width).astype(BF16)
        for qb in range(qblocks):
            for r in (0, 1):
                start = pl.multiple_of(m * 4 * SUB + r * 2 * SUB, 2 * SUB)
                held[qb, pl.ds(start, 2 * SUB), :] = both[r, qb]
        return carry

    lax.fori_loop(0, prow // 2, step, 0, unroll=16)

    def reduce_pair(x, y, lane, step):
        low = (lane // step) % 2 == 0
        if step >= team:
            return jnp.where(low, x, y)
        return jnp.where(low, x, y) + turn(jnp.where(low, y, x), step * share)

    whole_lane = lanes_of((prow * SUB, width)) // share
    for qb in range(0, qblocks, 2):
        seqs = [dot(last[...], held[qb + e]) for e in (0, 1)]
        taps_out[qb // 2] = reduce_pair(seqs[0][:, width:], seqs[1][:, width:], whole_lane, 1)
        ends = [x[:, :width].reshape(groups, blocks, SUB, width) for x in seqs]
        both = [
            jnp.concatenate([x[:, p] for x in ends], axis=1)
            .reshape(groups * 2 * SUB, width)
            .astype(BF16)
            for p in range(blocks)
        ]
        for p in range(blocks):
            post[qb // 2 * blocks + p] = skew(both[p], p, share)

    def store_out(g, a, b, x, y):
        rows = slice(g * 2 * SUB, (g + 1) * 2 * SUB)
        for i in range(groups):
            tile = slice(i * 2 * SUB, (i + 1) * 2 * SUB)
            out[seats[a][i], rows, :] = x[tile]
            out[seats[b][i], rows, :] = y[tile]

    regroup(range(qblocks // 2), blocks, share, None, store_out, post)
    lane = lanes_of((each, width)) // share
    for i in range(groups):
        rows = slice(i * each, (i + 1) * each)
        xs = [taps_out[g, rows, :] for g in range(qblocks // 2)]
        step = 2
        while len(xs) > 1:
            xs = [reduce_pair(x, y, lane, step) for x, y in zip(xs[::2], xs[1::2])]
            step *= 2
        halves = xs[0].reshape(blocks // 2, 2 * SUB, width).astype(BF16)
        for b in range(team):
            out[seats[b][i], qlen:, :] = halves[b % 2]


def post_kernel(
    recv, key, value, cot, gate_far, key_far, value_far, gate_out, key_out, value_out, hold, sems
):
    blocks, qlen, chans = key.shape
    width = recv.shape[2]
    share = width // (2 * blocks)
    span = min(chans, 128)
    per = span // share
    spans = chans // span
    parts = 2
    size = qlen // parts
    copies = []

    def load(g, a):
        part, m = g // spans, g % spans
        return recv[m * per + a, part * size : (part + 1) * size, :]

    def store_one(g, a, x):
        part, m = g // spans, g % spans
        rows = slice(part * size, (part + 1) * size)
        cols = slice(m * span, (m + 1) * span)
        if a < blocks:
            gate_out[a, rows, cols] = cot[a, rows, cols] * x
        else:
            p = a - blocks
            key_out[p, rows, cols] = x * value[p, rows, cols]
            value_out[p, rows, cols] = x * key[p, rows, cols]

    def store(g, a, b, x, y):
        store_one(g, a, x)
        store_one(g, b, y)
        if g % spans == spans - 1 and b == 2 * blocks - 1:
            part = g // spans
            rows = pl.ds(part * size, size)
            for i, (near, far) in enumerate(
                [(gate_out, gate_far), (key_out, key_far), (value_out, value_far)]
            ):
                copy = pltpu.make_async_copy(
                    near.at[:, rows], far.at[:, rows], sems.at[3 * part + i]
                )
                copy.start()
                copies.append(copy)

    if width == span:
        regroup(range(parts * spans), per, share, load, store, hold)
    else:
        for g in range(parts * spans):
            xs = gather_lanes([load(g, a) for a in range(per)], share)
            for a in range(0, 2 * blocks, 2):
                store(g, a, a + 1, xs[a], xs[a + 1])
    for copy in copies:
        copy.wait()


def finish_kernel(scale, mine, theirs, out, hold):
    blocks, qlen, chans = out.shape
    width = mine.shape[2]
    share = width // (qlen // SUB)
    span = min(chans, 128)
    per = span // share
    spans = chans // span
    flip = lax.rem(lax.axis_index("dp"), 2) == 0

    def load(g, a):
        c, m = g // spans, g % spans
        x, y = mine[m * per + a], theirs[m * per + a]
        return jnp.where(flip == (c == 0), x, y)

    def store(g, a, b, x, y):
        c, m = g // spans, g % spans
        ends = [z.astype(F32) * scale for z in (x, y)]
        for e in (0, 1):
            rows = slice(e * SUB, (e + 1) * SUB)
            both = jnp.concatenate([z[rows] for z in ends], axis=0).astype(BF16)
            out[2 * c + e, a * SUB : (a + 2) * SUB, m * span : (m + 1) * span] = both

    if width == span:
        regroup(range(2 * spans), per, share, load, store, hold)
    else:
        for g in range(2 * spans):
            xs = gather_lanes([load(g, a) for a in range(per)], share)
            for a in range(0, qlen // SUB, 2):
                store(g, a, a + 1, xs[a], xs[a + 1])


VM = pl.BlockSpec(memory_space=pltpu.VMEM)
FAR = pl.BlockSpec(memory_space=pltpu.HBM)


def call(kernel, ins, outs, scratch=(), name=None, flops=0, out_specs=None, in_specs=None):
    nbytes = sum(math.prod(x.shape) * 2 for x in [*ins, *outs])
    held = nbytes + sum(math.prod(x.shape) * 2 for x in scratch if x.dtype == BF16)
    held += sum(math.prod(x.shape) * 4 for x in scratch if x.dtype == F32)
    return pl.pallas_call(
        kernel,
        out_shape=outs if len(outs) > 1 else outs[0],
        in_specs=in_specs or [VM] * len(ins),
        out_specs=out_specs or ([VM] * len(outs) if len(outs) > 1 else VM),
        scratch_shapes=list(scratch),
        compiler_params=pltpu.CompilerParams(vmem_limit_bytes=held + SPARE),
        cost_estimate=pl.CostEstimate(flops=flops, bytes_accessed=nbytes, transcendentals=0),
        name=name,
    )(*ins)


def shaped(shape, dtype=BF16):
    return jax.ShapeDtypeStruct(shape, dtype)


def local(out_gate, key_gate, value_input, filter_taps, cotangent, block_live):
    ctx = lax.axis_size("ctx")
    dp = lax.axis_size("dp")
    team = TEAM
    tok, chans = key_gate.shape[1:]
    blocks = block_live.shape[1]
    qlen = tok // blocks
    prow = blocks * ctx
    qblocks = qlen // SUB
    share = chans // (ctx * team)
    width = 2 * team * share
    peers = team * ctx
    grid = (blocks, qlen, chans)
    halves = (2 * blocks * chans // min(chans, 128) * 2, qlen // 2, min(chans, 128))
    first, mid, back, last = transform_tables(prow, qlen)
    first, last = jnp.asarray(first), jnp.asarray(last)
    turns = jnp.asarray(np.concatenate([mid, back]))
    spread = jnp.asarray(spread_table(qblocks, 2 * team, share))
    order = np.arange(peers)
    random.Random(SEED).shuffle(order)
    seats = np.argsort(order).reshape(team, ctx).tolist()
    teams = [(start * ctx + order).tolist() for start in range(0, dp, team)]

    def trade(x, bit):
        return lax.ppermute(x, "dp", [(i, i ^ bit) for i in range(dp)])

    def exchange(x):
        return lax.all_to_all(
            x, ("dp", "ctx"), split_axis=0, concat_axis=0, tiled=True, axis_index_groups=teams
        )

    packed, key, value, cot = call(
        functools.partial(prep_kernel, team),
        [
            pltpu.with_memory_space_constraint(x, pltpu.HBM)
            for x in (
                block_live,
                out_gate.reshape(grid),
                key_gate.reshape(grid),
                value_input.reshape(grid),
                cotangent.reshape(grid),
                filter_taps.reshape(grid),
            )
        ],
        [shaped((peers, qlen + SUB, width))] + [shaped(grid)] * 3,
        scratch=[
            *[pltpu.VMEM(grid, BF16)] * 3,
            pltpu.VMEM((qlen, chans), BF16),
            pltpu.SMEM(block_live.shape, jnp.int32),
            pltpu.VMEM(halves, BF16),
            pltpu.VMEM((peers, SUB, width), F32),
            pltpu.SemaphoreType.DMA((10,)),
        ],
        in_specs=[FAR] * 6,
        name="gate_and_pack",
        flops=10**10,
    )
    tables = [first, spread, turns, last]
    outs = call(
        functools.partial(main_kernel, seats),
        [
            exchange(packed),
            *tables,
        ],
        [shaped((peers, qlen + 2 * SUB, width))],
        scratch=[
            pltpu.VMEM((qblocks, prow * SUB, 2 * width), BF16),
            pltpu.VMEM((prow * SUB, width), BF16),
            pltpu.VMEM((2 * prow, qlen, 2 * width), BF16),
            pltpu.VMEM((qblocks, 2 * prow * SUB, 2 * width), BF16),
            pltpu.VMEM((ctx * blocks, qlen, width), BF16),
            pltpu.VMEM((qblocks // 2 * blocks, ctx * 2 * SUB, width), BF16),
            pltpu.VMEM((qblocks // 2, prow * SUB, width), F32),
        ],
        name="convolve",
    )
    bit = team
    while bit < dp:
        part = outs[:, qlen:, :]
        total = part.astype(F32) + trade(part, bit).astype(F32)
        outs = lax.dynamic_update_slice(outs, total.astype(BF16), (0, qlen, 0))
        bit *= 2
    recv = exchange(outs)
    mine = recv[:, qlen:, :]
    theirs = trade(mine, 1)
    grads = call(
        post_kernel,
        [recv, key, value, cot],
        [shaped(grid)] * 3,
        scratch=[pltpu.VMEM(grid, BF16)] * 3
        + [pltpu.VMEM(halves, BF16), pltpu.SemaphoreType.DMA((6,))],
        out_specs=[FAR] * 3,
        name="ungate",
    )
    scale = 1.0 / math.sqrt(dp * tok * ctx)
    grad_taps = call(
        functools.partial(finish_kernel, scale),
        [mine, theirs],
        [shaped(grid)],
        scratch=[pltpu.VMEM((2 * peers, 2 * SUB, width), BF16)],
        name="scale_taps",
    )
    return (*[x.reshape(key_gate.shape) for x in grads], grad_taps.reshape(filter_taps.shape))


def solution(mesh):
    return jax.shard_map(
        local,
        mesh=mesh,
        in_specs=(
            P("dp", "ctx", None),
            P("dp", "ctx", None),
            P("dp", "ctx", None),
            P("ctx", None),
            P("dp", "ctx", None),
            P("dp", "ctx"),
        ),
        out_specs=(
            P("dp", "ctx", None),
            P("dp", "ctx", None),
            P("dp", "ctx", None),
            P("ctx", None),
        ),
        check_vma=False,
    )
```

```python
import functools
import itertools
import math
import random

import jax
import jax.numpy as jnp
import ml_dtypes
import numpy as np
from jax import lax
from jax.experimental import pallas as pl
from jax.experimental.pallas import tpu as pltpu
from jax.sharding import PartitionSpec as P


SUB = 8
TEAM = 4
SEED = 84
SPARE = 4 * 1024 * 1024
F32 = jnp.float32
BF16 = jnp.bfloat16


def transform_tables(prow, qlen):
    total = prow * qlen
    k1 = np.arange(prow)
    p = np.arange(prow)
    theta = 2.0 * np.pi * (((4 * k1[:, None] + 1) * p[None, :]) % (4 * prow)) / (4 * prow)
    eye = np.eye(SUB)
    first = np.stack([np.cos(theta), -np.sin(theta)], axis=1)
    first = np.einsum("krp,ab->krapb", first, eye).reshape(prow * 2 * SUB, prow * SUB)
    last = np.stack([np.cos(theta), -np.sin(theta)], axis=0) / total
    last = last.reshape(2, prow // 2, 2, prow)
    last = np.einsum("rmlp,ab->pamrlb", last, eye).reshape(prow * SUB, prow * 2 * SUB)
    q = np.arange(qlen)
    k2 = np.arange(qlen)
    phase = (4 * k1[:, None, None] + 1 + 4 * prow * k2[None, :, None]) * q[None, None, :]
    phi = 2.0 * np.pi * (phase % (4 * total)) / (4 * total)
    re, im = np.cos(phi), -np.sin(phi)
    mid = np.concatenate(
        [np.concatenate([re, -im], axis=2), np.concatenate([im, re], axis=2)], axis=1
    )
    back = np.swapaxes(mid, 1, 2)
    return [t.astype(ml_dtypes.bfloat16) for t in (first, mid, back, last)]


def spread_table(qblocks, copies, share):
    spread = np.einsum("ab,cd,e->acbed", np.eye(qblocks), np.eye(share), np.ones(copies))
    return spread.reshape(qblocks * share, -1).astype(ml_dtypes.bfloat16)


def dot(a, b):
    return jnp.dot(a, b, preferred_element_type=F32)


def turn(x, shift):
    width = x.shape[-1]
    shift %= width
    if width == 128:
        return pltpu.roll(x, shift, 1)
    return jnp.concatenate([x[:, width - shift :], x[:, : width - shift]], axis=1)


def lanes_of(shape):
    return lax.broadcasted_iota(jnp.int32, shape, len(shape) - 1)


def skew(x, a, unit):
    return turn(x, unit * a) if a else x


def regroup(groups, count, unit, load, store, hold):
    if load is not None:
        for g in groups:
            for a in range(count):
                hold[g * count + a] = skew(load(g, a), a, unit)
    for g in groups:
        xs = [hold[g * count + (-k) % count] for k in range(count)]
        block = lanes_of(xs[0].shape) // unit
        step = 1
        while step < count:
            moved = (block // step) % 2 == 1
            xs = [jnp.where(moved, xs[b - step], xs[b]) for b in range(count)]
            step *= 2
        xs = [skew(x, -b, unit) for b, x in enumerate(xs)]
        for b in range(0, count, 2):
            store(g, b, b + 1, xs[b], xs[b + 1])


def gather_lanes(xs, unit):
    return [
        jnp.concatenate([x[:, k * unit : (k + 1) * unit] for x in xs], axis=1)
        for k in range(xs[0].shape[1] // unit)
    ]


def prep_kernel(
    team, live_far, out_gate_far, key_far, value_far, cot_far, taps_far,
    out, key_out, value_out, cot, key, value, out_gate, taps, live, hold, hold_taps, sems,
):
    blocks, qlen, chans = key.shape
    lanes = out.shape[2]
    share = lanes // (2 * blocks)
    span = min(chans, 128)
    per = span // share
    spans = chans // span
    place = lax.rem(lax.axis_index("dp"), team)
    parts = 2
    size = qlen // parts
    taps_copy = pltpu.make_async_copy(taps_far.at[place], taps, sems.at[0])
    live_copy = pltpu.make_async_copy(live_far, live, sems.at[1])
    copies = []
    for part in range(parts):
        rows = pl.ds(part * size, size)
        copies.append([
            pltpu.make_async_copy(far.at[:, rows], near.at[:, rows], sems.at[2 + 4 * part + i])
            for i, (far, near) in enumerate(
                [(key_far, key), (value_far, value), (cot_far, cot), (out_gate_far, out_gate)]
            )
        ])
    taps_copy.start()
    live_copy.start()
    for group in copies:
        for copy in group:
            copy.start()

    def load(g, a):
        part, m = g // spans, g % spans
        if lanes == span and a == 0 and m == 0:
            for copy in copies[part]:
                copy.wait()
        p = a % blocks
        rows = slice(part * size, (part + 1) * size)
        cols = slice(m * span, (m + 1) * span)
        if a >= blocks:
            return cot[p, rows, cols] * out_gate[p, rows, cols]
        dead = live[0, p] == 0
        none = jnp.zeros((size, span), BF16)
        kept = jnp.where(dead, none, key[p, rows, cols])
        kept_value = jnp.where(dead, none, value[p, rows, cols])
        key_out[p, rows, cols] = kept
        value_out[p, rows, cols] = kept_value
        return kept * kept_value

    def store(g, a, b, x, y):
        part, m = g // spans, g % spans
        rows = slice(part * size, (part + 1) * size)
        out[m * per + a, rows, :] = x
        out[m * per + b, rows, :] = y

    def load_taps(g, a):
        return taps[a * SUB : (a + 1) * SUB, g * span : (g + 1) * span].astype(F32)

    def store_taps(g, a, b, x, y):
        out[g * per + a, qlen:, :] = x.astype(BF16)
        out[g * per + b, qlen:, :] = y.astype(BF16)

    if lanes == span:
        taps_copy.wait()
        regroup(range(spans), qlen // SUB, share, load_taps, store_taps, hold_taps)
        live_copy.wait()
        regroup(range(parts * spans), 2 * blocks, share, load, store, hold)
    else:
        for copy in [taps_copy, live_copy, *itertools.chain(*copies)]:
            copy.wait()
        for g in range(parts * spans):
            xs = gather_lanes([load(g, a) for a in range(2 * blocks)], share)
            for k in range(0, per, 2):
                store(g, k, k + 1, xs[k], xs[k + 1])
        for g in range(spans):
            xs = gather_lanes([load_taps(g, a) for a in range(qlen // SUB)], share)
            for k in range(0, per, 2):
                store_taps(g, k, k + 1, xs[k], xs[k + 1])


def pair_tiles(a, b, qblocks):
    width = a.shape[1]
    ends = [x.reshape(qblocks, 1, SUB, width) for x in (a, b)]
    return jnp.concatenate(ends, axis=1).reshape(qblocks, 2 * SUB, width).astype(BF16)


def main_kernel(
    seats, recv, first, spread, turns, last,
    out, signal_held, taps_held, rows_held, held, hold, post, taps_out,
):
    full_rows, width = recv.shape[1:]
    prow = turns.shape[0] // 2
    qlen = turns.shape[1] // 2
    qblocks = qlen // SUB
    team = qblocks // 2
    groups = recv.shape[0] // team
    blocks = prow // groups
    each = blocks * SUB
    share = width // qblocks

    for i in range(groups):
        for p in range(0, blocks, 2):
            rows = slice(i * each + p * SUB, i * each + (p + 2) * SUB)
            ends = [recv[seats[p + e][i], qlen:, :].astype(F32) for e in (0, 1)]
            taps_held[rows, :] = jnp.concatenate(ends, axis=0).astype(BF16)

    def load(i, b):
        return recv[seats[b][i], :qlen, :]

    def store(i, a, b, x, y):
        rows = slice(i * each + a * SUB, i * each + (a + 2) * SUB)
        signal_held[:, rows, :width] = pair_tiles(x.astype(F32), y.astype(F32), qblocks)

    regroup(range(groups), blocks, share, load, store, hold)
    for qb in range(qblocks):
        table = spread[:, qb * width : (qb + 1) * width]
        signal_held[qb, :, width:] = dot(taps_held[...], table).astype(BF16)
    for qb in range(0, qblocks, 2):
        ends = [
            dot(first[...], signal_held[qb + e]).reshape(2 * prow, SUB, 2 * width) for e in (0, 1)
        ]
        rows_held[:, qb * SUB : (qb + 2) * SUB, :] = jnp.concatenate(ends, axis=1).astype(BF16)

    low = lanes_of((qlen, width)) < width // 2

    def step(m, carry):
        ends = []
        for e in (0, 1):
            k1 = 2 * m + e
            rows = rows_held[pl.ds(2 * k1, 2)].reshape(2 * qlen, 2 * width)
            full = dot(turns[k1], rows)
            re, im = full[:qlen, :width], full[qlen:, :width]
            hre, him = full[:qlen, width:], full[qlen:, width:]
            him = jnp.where(low, him, -him)
            ore, oim = turn(re, width // 2), turn(im, width // 2)
            tim = im * ore - re * oim
            real = jnp.concatenate([re * hre - im * him, re * ore + im * oim], axis=1)
            imag = jnp.concatenate([re * him + im * hre, jnp.where(low, -tim, tim)], axis=1)
            both = jnp.concatenate([real, imag], axis=0).astype(BF16)
            ends.append(dot(turns[prow + k1], both))
        parts = [x.reshape(2, qblocks, 1, SUB, 2 * width) for x in ends]
        both = jnp.concatenate(parts, axis=2).reshape(2, qblocks, 2 * SUB, 2 * width).astype(BF16)
        for qb in range(qblocks):
            for r in (0, 1):
                start = pl.multiple_of(m * 4 * SUB + r * 2 * SUB, 2 * SUB)
                held[qb, pl.ds(start, 2 * SUB), :] = both[r, qb]
        return carry

    lax.fori_loop(0, prow // 2, step, 0, unroll=16)

    def reduce_pair(x, y, lane, step):
        low = (lane // step) % 2 == 0
        if step >= team:
            return jnp.where(low, x, y)
        return jnp.where(low, x, y) + turn(jnp.where(low, y, x), step * share)

    whole_lane = lanes_of((prow * SUB, width)) // share
    for qb in range(0, qblocks, 2):
        seqs = [dot(last[...], held[qb + e]) for e in (0, 1)]
        taps_out[qb // 2] = reduce_pair(seqs[0][:, width:], seqs[1][:, width:], whole_lane, 1)
        ends = [x[:, :width].reshape(groups, blocks, SUB, width) for x in seqs]
        both = [
            jnp.concatenate([x[:, p] for x in ends], axis=1)
            .reshape(groups * 2 * SUB, width)
            .astype(BF16)
            for p in range(blocks)
        ]
        for p in range(blocks):
            post[qb // 2 * blocks + p] = skew(both[p], p, share)

    def store_out(g, a, b, x, y):
        rows = slice(g * 2 * SUB, (g + 1) * 2 * SUB)
        for i in range(groups):
            tile = slice(i * 2 * SUB, (i + 1) * 2 * SUB)
            out[seats[a][i], rows, :] = x[tile]
            out[seats[b][i], rows, :] = y[tile]

    regroup(range(qblocks // 2), blocks, share, None, store_out, post)
    lane = lanes_of((each, width)) // share
    for i in range(groups):
        rows = slice(i * each, (i + 1) * each)
        xs = [taps_out[g, rows, :] for g in range(qblocks // 2)]
        step = 2
        while len(xs) > 1:
            xs = [reduce_pair(x, y, lane, step) for x, y in zip(xs[::2], xs[1::2])]
            step *= 2
        halves = xs[0].reshape(blocks // 2, 2 * SUB, width).astype(BF16)
        for b in range(team):
            out[seats[b][i], qlen:, :] = halves[b % 2]


def post_kernel(
    recv, key, value, cot, gate_far, key_far, value_far, gate_out, key_out, value_out, hold, sems
):
    blocks, qlen, chans = key.shape
    width = recv.shape[2]
    share = width // (2 * blocks)
    span = min(chans, 128)
    per = span // share
    spans = chans // span
    parts = 2
    size = qlen // parts
    copies = []

    def load(g, a):
        part, m = g // spans, g % spans
        return recv[m * per + a, part * size : (part + 1) * size, :]

    def store_one(g, a, x):
        part, m = g // spans, g % spans
        rows = slice(part * size, (part + 1) * size)
        cols = slice(m * span, (m + 1) * span)
        if a < blocks:
            gate_out[a, rows, cols] = cot[a, rows, cols] * x
        else:
            p = a - blocks
            key_out[p, rows, cols] = x * value[p, rows, cols]
            value_out[p, rows, cols] = x * key[p, rows, cols]

    def store(g, a, b, x, y):
        store_one(g, a, x)
        store_one(g, b, y)
        if g % spans == spans - 1 and b == 2 * blocks - 1:
            part = g // spans
            rows = pl.ds(part * size, size)
            for i, (near, far) in enumerate(
                [(gate_out, gate_far), (key_out, key_far), (value_out, value_far)]
            ):
                copy = pltpu.make_async_copy(
                    near.at[:, rows], far.at[:, rows], sems.at[3 * part + i]
                )
                copy.start()
                copies.append(copy)

    if width == span:
        regroup(range(parts * spans), per, share, load, store, hold)
    else:
        for g in range(parts * spans):
            xs = gather_lanes([load(g, a) for a in range(per)], share)
            for a in range(0, 2 * blocks, 2):
                store(g, a, a + 1, xs[a], xs[a + 1])
    for copy in copies:
        copy.wait()


def finish_kernel(scale, mine, theirs, out, hold):
    blocks, qlen, chans = out.shape
    width = mine.shape[2]
    share = width // (qlen // SUB)
    span = min(chans, 128)
    per = span // share
    spans = chans // span
    flip = lax.rem(lax.axis_index("dp"), 2) == 0

    def load(g, a):
        c, m = g // spans, g % spans
        x, y = mine[m * per + a], theirs[m * per + a]
        return jnp.where(flip == (c == 0), x, y)

    def store(g, a, b, x, y):
        c, m = g // spans, g % spans
        ends = [z.astype(F32) * scale for z in (x, y)]
        for e in (0, 1):
            rows = slice(e * SUB, (e + 1) * SUB)
            both = jnp.concatenate([z[rows] for z in ends], axis=0).astype(BF16)
            out[2 * c + e, a * SUB : (a + 2) * SUB, m * span : (m + 1) * span] = both

    if width == span:
        regroup(range(2 * spans), per, share, load, store, hold)
    else:
        for g in range(2 * spans):
            xs = gather_lanes([load(g, a) for a in range(per)], share)
            for a in range(0, qlen // SUB, 2):
                store(g, a, a + 1, xs[a], xs[a + 1])


VM = pl.BlockSpec(memory_space=pltpu.VMEM)
FAR = pl.BlockSpec(memory_space=pltpu.HBM)


def call(kernel, ins, outs, scratch=(), name=None, flops=0, out_specs=None, in_specs=None):
    nbytes = sum(math.prod(x.shape) * 2 for x in [*ins, *outs])
    held = nbytes + sum(math.prod(x.shape) * 2 for x in scratch if x.dtype == BF16)
    held += sum(math.prod(x.shape) * 4 for x in scratch if x.dtype == F32)
    return pl.pallas_call(
        kernel,
        out_shape=outs if len(outs) > 1 else outs[0],
        in_specs=in_specs or [VM] * len(ins),
        out_specs=out_specs or ([VM] * len(outs) if len(outs) > 1 else VM),
        scratch_shapes=list(scratch),
        compiler_params=pltpu.CompilerParams(vmem_limit_bytes=held + SPARE),
        cost_estimate=pl.CostEstimate(flops=flops, bytes_accessed=nbytes, transcendentals=0),
        name=name,
    )(*ins)


def shaped(shape, dtype=BF16):
    return jax.ShapeDtypeStruct(shape, dtype)


def local(out_gate, key_gate, value_input, filter_taps, cotangent, block_live):
    ctx = lax.axis_size("ctx")
    dp = lax.axis_size("dp")
    team = TEAM
    tok, chans = key_gate.shape[1:]
    blocks = block_live.shape[1]
    qlen = tok // blocks
    prow = blocks * ctx
    qblocks = qlen // SUB
    share = chans // (ctx * team)
    width = 2 * team * share
    peers = team * ctx
    grid = (blocks, qlen, chans)
    halves = (2 * blocks * chans // min(chans, 128) * 2, qlen // 2, min(chans, 128))
    first, mid, back, last = transform_tables(prow, qlen)
    first, last = jnp.asarray(first), jnp.asarray(last)
    turns = jnp.asarray(np.concatenate([mid, back]))
    spread = jnp.asarray(spread_table(qblocks, 2 * team, share))
    order = np.arange(peers)
    random.Random(SEED).shuffle(order)
    seats = np.argsort(order).reshape(team, ctx).tolist()
    teams = [(start * ctx + order).tolist() for start in range(0, dp, team)]

    def trade(x, bit):
        return lax.ppermute(x, "dp", [(i, i ^ bit) for i in range(dp)])

    def exchange(x):
        return lax.all_to_all(
            x, ("dp", "ctx"), split_axis=0, concat_axis=0, tiled=True, axis_index_groups=teams
        )

    packed, key, value, cot = call(
        functools.partial(prep_kernel, team),
        [
            pltpu.with_memory_space_constraint(x, pltpu.HBM)
            for x in (
                block_live,
                out_gate.reshape(grid),
                key_gate.reshape(grid),
                value_input.reshape(grid),
                cotangent.reshape(grid),
                filter_taps.reshape(grid),
            )
        ],
        [shaped((peers, qlen + SUB, width))] + [shaped(grid)] * 3,
        scratch=[
            *[pltpu.VMEM(grid, BF16)] * 3,
            pltpu.VMEM((qlen, chans), BF16),
            pltpu.SMEM(block_live.shape, jnp.int32),
            pltpu.VMEM(halves, BF16),
            pltpu.VMEM((peers, SUB, width), F32),
            pltpu.SemaphoreType.DMA((10,)),
        ],
        in_specs=[FAR] * 6,
        name="gate_and_pack",
        flops=10**10,
    )
    tables = [first, spread, turns, last]
    outs = call(
        functools.partial(main_kernel, seats),
        [
            exchange(packed),
            *tables,
        ],
        [shaped((peers, qlen + 2 * SUB, width))],
        scratch=[
            pltpu.VMEM((qblocks, prow * SUB, 2 * width), BF16),
            pltpu.VMEM((prow * SUB, width), BF16),
            pltpu.VMEM((2 * prow, qlen, 2 * width), BF16),
            pltpu.VMEM((qblocks, 2 * prow * SUB, 2 * width), BF16),
            pltpu.VMEM((ctx * blocks, qlen, width), BF16),
            pltpu.VMEM((qblocks // 2 * blocks, ctx * 2 * SUB, width), BF16),
            pltpu.VMEM((qblocks // 2, prow * SUB, width), F32),
        ],
        name="convolve",
    )
    bit = team
    while bit < dp:
        part = outs[:, qlen:, :]
        total = part.astype(F32) + trade(part, bit).astype(F32)
        outs = lax.dynamic_update_slice(outs, total.astype(BF16), (0, qlen, 0))
        bit *= 2
    recv = exchange(outs)
    mine = recv[:, qlen:, :]
    theirs = trade(mine, 1)
    grads = call(
        post_kernel,
        [recv, key, value, cot],
        [shaped(grid)] * 3,
        scratch=[pltpu.VMEM(grid, BF16)] * 3
        + [pltpu.VMEM(halves, BF16), pltpu.SemaphoreType.DMA((6,))],
        out_specs=[FAR] * 3,
        name="ungate",
    )
    scale = 1.0 / math.sqrt(dp * tok * ctx)
    grad_taps = call(
        functools.partial(finish_kernel, scale),
        [mine, theirs],
        [shaped(grid)],
        scratch=[pltpu.VMEM((2 * peers, 2 * SUB, width), BF16)],
        name="scale_taps",
    )
    return (*[x.reshape(key_gate.shape) for x in grads], grad_taps.reshape(filter_taps.shape))


def solution(mesh):
    return jax.shard_map(
        local,
        mesh=mesh,
        in_specs=(
            P("dp", "ctx", None),
            P("dp", "ctx", None),
            P("dp", "ctx", None),
            P("ctx", None),
            P("dp", "ctx", None),
            P("dp", "ctx"),
        ),
        out_specs=(
            P("dp", "ctx", None),
            P("dp", "ctx", None),
            P("dp", "ctx", None),
            P("ctx", None),
        ),
        check_vma=False,
    )
```

```python
import functools
import itertools
import math
import random

import jax
import jax.numpy as jnp
import ml_dtypes
import numpy as np
from jax import lax
from jax.experimental import pallas as pl
from jax.experimental.pallas import tpu as pltpu
from jax.sharding import PartitionSpec as P


SUB = 8
TEAM = 4
SEED = 139
SPARE = 4 * 1024 * 1024
F32 = jnp.float32
BF16 = jnp.bfloat16


def transform_tables(prow, qlen):
    total = prow * qlen
    k1 = np.arange(prow)
    p = np.arange(prow)
    theta = 2.0 * np.pi * (((4 * k1[:, None] + 1) * p[None, :]) % (4 * prow)) / (4 * prow)
    eye = np.eye(SUB)
    first = np.stack([np.cos(theta), -np.sin(theta)], axis=1)
    first = np.einsum("krp,ab->krapb", first, eye).reshape(prow * 2 * SUB, prow * SUB)
    last = np.stack([np.cos(theta), -np.sin(theta)], axis=0) / total
    last = last.reshape(2, prow // 2, 2, prow)
    last = np.einsum("rmlp,ab->pamrlb", last, eye).reshape(prow * SUB, prow * 2 * SUB)
    q = np.arange(qlen)
    k2 = np.arange(qlen)
    phase = (4 * k1[:, None, None] + 1 + 4 * prow * k2[None, :, None]) * q[None, None, :]
    phi = 2.0 * np.pi * (phase % (4 * total)) / (4 * total)
    re, im = np.cos(phi), -np.sin(phi)
    mid = np.concatenate(
        [np.concatenate([re, -im], axis=2), np.concatenate([im, re], axis=2)], axis=1
    )
    back = np.swapaxes(mid, 1, 2)
    return [t.astype(ml_dtypes.bfloat16) for t in (first, mid, back, last)]


def spread_table(qblocks, copies, share):
    spread = np.einsum("ab,cd,e->acbed", np.eye(qblocks), np.eye(share), np.ones(copies))
    return spread.reshape(qblocks * share, -1).astype(ml_dtypes.bfloat16)


def dot(a, b):
    return jnp.dot(a, b, preferred_element_type=F32)


def turn(x, shift):
    width = x.shape[-1]
    shift %= width
    if width == 128:
        return pltpu.roll(x, shift, 1)
    return jnp.concatenate([x[:, width - shift :], x[:, : width - shift]], axis=1)


def lanes_of(shape):
    return lax.broadcasted_iota(jnp.int32, shape, len(shape) - 1)


def skew(x, a, unit):
    return turn(x, unit * a) if a else x


def regroup(groups, count, unit, load, store, hold):
    if load is not None:
        for g in groups:
            for a in range(count):
                hold[g * count + a] = skew(load(g, a), a, unit)
    for g in groups:
        xs = [hold[g * count + (-k) % count] for k in range(count)]
        block = lanes_of(xs[0].shape) // unit
        step = 1
        while step < count:
            moved = (block // step) % 2 == 1
            xs = [jnp.where(moved, xs[b - step], xs[b]) for b in range(count)]
            step *= 2
        xs = [skew(x, -b, unit) for b, x in enumerate(xs)]
        for b in range(0, count, 2):
            store(g, b, b + 1, xs[b], xs[b + 1])


def gather_lanes(xs, unit):
    return [
        jnp.concatenate([x[:, k * unit : (k + 1) * unit] for x in xs], axis=1)
        for k in range(xs[0].shape[1] // unit)
    ]


def prep_kernel(
    team, live_far, out_gate_far, key_far, value_far, cot_far, taps_far,
    out, key_out, value_out, cot, key, value, out_gate, taps, live, hold, hold_taps, sems,
):
    blocks, qlen, chans = key.shape
    lanes = out.shape[2]
    share = lanes // (2 * blocks)
    span = min(chans, 128)
    per = span // share
    spans = chans // span
    place = lax.rem(lax.axis_index("dp"), team)
    parts = 2
    size = qlen // parts
    taps_copy = pltpu.make_async_copy(taps_far.at[place], taps, sems.at[0])
    live_copy = pltpu.make_async_copy(live_far, live, sems.at[1])
    copies = []
    for part in range(parts):
        rows = pl.ds(part * size, size)
        copies.append([
            pltpu.make_async_copy(far.at[:, rows], near.at[:, rows], sems.at[2 + 4 * part + i])
            for i, (far, near) in enumerate(
                [(key_far, key), (value_far, value), (cot_far, cot), (out_gate_far, out_gate)]
            )
        ])
    taps_copy.start()
    live_copy.start()
    for group in copies:
        for copy in group:
            copy.start()

    def load(g, a):
        part, m = g // spans, g % spans
        if lanes == span and a == 0 and m == 0:
            for copy in copies[part]:
                copy.wait()
        p = a % blocks
        rows = slice(part * size, (part + 1) * size)
        cols = slice(m * span, (m + 1) * span)
        if a >= blocks:
            return cot[p, rows, cols] * out_gate[p, rows, cols]
        dead = live[0, p] == 0
        none = jnp.zeros((size, span), BF16)
        kept = jnp.where(dead, none, key[p, rows, cols])
        kept_value = jnp.where(dead, none, value[p, rows, cols])
        key_out[p, rows, cols] = kept
        value_out[p, rows, cols] = kept_value
        return kept * kept_value

    def store(g, a, b, x, y):
        part, m = g // spans, g % spans
        rows = slice(part * size, (part + 1) * size)
        out[m * per + a, rows, :] = x
        out[m * per + b, rows, :] = y

    def load_taps(g, a):
        return taps[a * SUB : (a + 1) * SUB, g * span : (g + 1) * span].astype(F32)

    def store_taps(g, a, b, x, y):
        out[g * per + a, qlen:, :] = x.astype(BF16)
        out[g * per + b, qlen:, :] = y.astype(BF16)

    if lanes == span:
        taps_copy.wait()
        regroup(range(spans), qlen // SUB, share, load_taps, store_taps, hold_taps)
        live_copy.wait()
        regroup(range(parts * spans), 2 * blocks, share, load, store, hold)
    else:
        for copy in [taps_copy, live_copy, *itertools.chain(*copies)]:
            copy.wait()
        for g in range(parts * spans):
            xs = gather_lanes([load(g, a) for a in range(2 * blocks)], share)
            for k in range(0, per, 2):
                store(g, k, k + 1, xs[k], xs[k + 1])
        for g in range(spans):
            xs = gather_lanes([load_taps(g, a) for a in range(qlen // SUB)], share)
            for k in range(0, per, 2):
                store_taps(g, k, k + 1, xs[k], xs[k + 1])


def pair_tiles(a, b, qblocks):
    width = a.shape[1]
    ends = [x.reshape(qblocks, 1, SUB, width) for x in (a, b)]
    return jnp.concatenate(ends, axis=1).reshape(qblocks, 2 * SUB, width).astype(BF16)


def main_kernel(
    seats, recv, first, spread, turns, last,
    out, signal_held, taps_held, rows_held, held, hold, post, taps_out,
):
    full_rows, width = recv.shape[1:]
    prow = turns.shape[0] // 2
    qlen = turns.shape[1] // 2
    qblocks = qlen // SUB
    team = qblocks // 2
    groups = recv.shape[0] // team
    blocks = prow // groups
    each = blocks * SUB
    share = width // qblocks

    for i in range(groups):
        for p in range(0, blocks, 2):
            rows = slice(i * each + p * SUB, i * each + (p + 2) * SUB)
            ends = [recv[seats[p + e][i], qlen:, :].astype(F32) for e in (0, 1)]
            taps_held[rows, :] = jnp.concatenate(ends, axis=0).astype(BF16)

    def load(i, b):
        return recv[seats[b][i], :qlen, :]

    def store(i, a, b, x, y):
        rows = slice(i * each + a * SUB, i * each + (a + 2) * SUB)
        signal_held[:, rows, :width] = pair_tiles(x.astype(F32), y.astype(F32), qblocks)

    regroup(range(groups), blocks, share, load, store, hold)
    for qb in range(qblocks):
        table = spread[:, qb * width : (qb + 1) * width]
        signal_held[qb, :, width:] = dot(taps_held[...], table).astype(BF16)
    for qb in range(0, qblocks, 2):
        ends = [
            dot(first[...], signal_held[qb + e]).reshape(2 * prow, SUB, 2 * width) for e in (0, 1)
        ]
        rows_held[:, qb * SUB : (qb + 2) * SUB, :] = jnp.concatenate(ends, axis=1).astype(BF16)

    low = lanes_of((qlen, width)) < width // 2

    def step(m, carry):
        ends = []
        for e in (0, 1):
            k1 = 2 * m + e
            rows = rows_held[pl.ds(2 * k1, 2)].reshape(2 * qlen, 2 * width)
            full = dot(turns[k1], rows)
            re, im = full[:qlen, :width], full[qlen:, :width]
            hre, him = full[:qlen, width:], full[qlen:, width:]
            him = jnp.where(low, him, -him)
            ore, oim = turn(re, width // 2), turn(im, width // 2)
            tim = im * ore - re * oim
            real = jnp.concatenate([re * hre - im * him, re * ore + im * oim], axis=1)
            imag = jnp.concatenate([re * him + im * hre, jnp.where(low, -tim, tim)], axis=1)
            both = jnp.concatenate([real, imag], axis=0).astype(BF16)
            ends.append(dot(turns[prow + k1], both))
        parts = [x.reshape(2, qblocks, 1, SUB, 2 * width) for x in ends]
        both = jnp.concatenate(parts, axis=2).reshape(2, qblocks, 2 * SUB, 2 * width).astype(BF16)
        for qb in range(qblocks):
            for r in (0, 1):
                start = pl.multiple_of(m * 4 * SUB + r * 2 * SUB, 2 * SUB)
                held[qb, pl.ds(start, 2 * SUB), :] = both[r, qb]
        return carry

    lax.fori_loop(0, prow // 2, step, 0, unroll=16)

    def reduce_pair(x, y, lane, step):
        low = (lane // step) % 2 == 0
        if step >= team:
            return jnp.where(low, x, y)
        return jnp.where(low, x, y) + turn(jnp.where(low, y, x), step * share)

    whole_lane = lanes_of((prow * SUB, width)) // share
    for qb in range(0, qblocks, 2):
        seqs = [dot(last[...], held[qb + e]) for e in (0, 1)]
        taps_out[qb // 2] = reduce_pair(seqs[0][:, width:], seqs[1][:, width:], whole_lane, 1)
        ends = [x[:, :width].reshape(groups, blocks, SUB, width) for x in seqs]
        both = [
            jnp.concatenate([x[:, p] for x in ends], axis=1)
            .reshape(groups * 2 * SUB, width)
            .astype(BF16)
            for p in range(blocks)
        ]
        for p in range(blocks):
            post[qb // 2 * blocks + p] = skew(both[p], p, share)

    def store_out(g, a, b, x, y):
        rows = slice(g * 2 * SUB, (g + 1) * 2 * SUB)
        for i in range(groups):
            tile = slice(i * 2 * SUB, (i + 1) * 2 * SUB)
            out[seats[a][i], rows, :] = x[tile]
            out[seats[b][i], rows, :] = y[tile]

    regroup(range(qblocks // 2), blocks, share, None, store_out, post)
    lane = lanes_of((each, width)) // share
    for i in range(groups):
        rows = slice(i * each, (i + 1) * each)
        xs = [taps_out[g, rows, :] for g in range(qblocks // 2)]
        step = 2
        while len(xs) > 1:
            xs = [reduce_pair(x, y, lane, step) for x, y in zip(xs[::2], xs[1::2])]
            step *= 2
        halves = xs[0].reshape(blocks // 2, 2 * SUB, width).astype(BF16)
        for b in range(team):
            out[seats[b][i], qlen:, :] = halves[b % 2]


def restore_taps(load, scale, stage, hold):
    _, qlen, chans = stage.shape
    width = hold.shape[2]
    share = width // (qlen // SUB)
    span = min(chans, 128)
    per = span // share

    def load_one(g, a):
        return load(g * per + a)

    def store(g, a, b, x, y):
        ends = [z.astype(F32) * scale for z in (x, y)]
        for e in (0, 1):
            rows = slice(e * SUB, (e + 1) * SUB)
            both = jnp.concatenate([z[rows] for z in ends], axis=0).astype(BF16)
            stage[e, a * SUB : (a + 2) * SUB, g * span : (g + 1) * span] = both

    if width == span:
        regroup(range(chans // span), per, share, load_one, store, hold)
    else:
        for g in range(chans // span):
            xs = gather_lanes([load_one(g, a) for a in range(per)], share)
            for a in range(0, qlen // SUB, 2):
                store(g, a, a + 1, xs[a], xs[a + 1])


def core_half(core):
    return pl.ds(pl.multiple_of(2 * core, 2), 2)


def post_kernel(
    scale, recv, key, value, cot, gate_far, key_far, value_far, taps_far,
    gate_out, key_out, value_out, stage, hold, hold_taps, sems,
):
    core = lax.rem(lax.axis_index("dp"), 2)
    blocks, qlen, chans = key.shape
    width = recv.shape[2]
    share = width // (2 * blocks)
    span = min(chans, 128)
    per = span // share
    spans = chans // span
    parts = 2
    size = qlen // parts
    copies = []

    def load(g, a):
        part, m = g // spans, g % spans
        return recv[m * per + a, part * size : (part + 1) * size, :]

    def store_one(g, a, x):
        part, m = g // spans, g % spans
        rows = slice(part * size, (part + 1) * size)
        cols = slice(m * span, (m + 1) * span)
        if a < blocks:
            gate_out[a, rows, cols] = cot[a, rows, cols] * x
        else:
            p = a - blocks
            key_out[p, rows, cols] = x * value[p, rows, cols]
            value_out[p, rows, cols] = x * key[p, rows, cols]

    def store(g, a, b, x, y):
        store_one(g, a, x)
        store_one(g, b, y)
        if g % spans == spans - 1 and b == 2 * blocks - 1:
            part = g // spans
            rows = pl.ds(part * size, size)
            for i, (near, far) in enumerate(
                [(gate_out, gate_far), (key_out, key_far), (value_out, value_far)]
            ):
                copy = pltpu.make_async_copy(
                    near.at[:, rows], far.at[:, rows], sems.at[3 * part + i]
                )
                copy.start()
                copies.append(copy)

    if width == span:
        regroup(range(parts * spans), per, share, load, store, hold)
    else:
        for g in range(parts * spans):
            xs = gather_lanes([load(g, a) for a in range(per)], share)
            for a in range(0, 2 * blocks, 2):
                store(g, a, a + 1, xs[a], xs[a + 1])
    restore_taps(lambda k: recv[k, qlen:, :], scale, stage, hold_taps)
    copy = pltpu.make_async_copy(stage, taps_far.at[core_half(core)], sems.at[3 * parts])
    copy.start()
    copies.append(copy)
    for copy in copies:
        copy.wait()


def finish_kernel(scale, theirs, begun, taps_far, stage, hold, sem):
    other = 1 - lax.rem(lax.axis_index("dp"), 2)
    restore_taps(lambda k: theirs[k], scale, stage, hold)
    copy = pltpu.make_async_copy(stage, taps_far.at[core_half(other)], sem.at[0])
    copy.start()
    copy.wait()


VM = pl.BlockSpec(memory_space=pltpu.VMEM)
FAR = pl.BlockSpec(memory_space=pltpu.HBM)


def call(kernel, ins, outs, scratch=(), name=None, flops=0, aliases=None, out_specs=None, in_specs=None):
    nbytes = sum(math.prod(x.shape) * 2 for x in [*ins, *outs])
    held = nbytes + sum(math.prod(x.shape) * 2 for x in scratch if x.dtype == BF16)
    held += sum(math.prod(x.shape) * 4 for x in scratch if x.dtype == F32)
    return pl.pallas_call(
        kernel,
        out_shape=outs if len(outs) > 1 else outs[0],
        in_specs=in_specs or [VM] * len(ins),
        out_specs=out_specs or ([VM] * len(outs) if len(outs) > 1 else VM),
        scratch_shapes=list(scratch),
        input_output_aliases=aliases or {},
        compiler_params=pltpu.CompilerParams(vmem_limit_bytes=held + SPARE),
        cost_estimate=pl.CostEstimate(flops=flops, bytes_accessed=nbytes, transcendentals=0),
        name=name,
    )(*ins)


def shaped(shape, dtype=BF16):
    return jax.ShapeDtypeStruct(shape, dtype)


def local(out_gate, key_gate, value_input, filter_taps, cotangent, block_live):
    ctx = lax.axis_size("ctx")
    dp = lax.axis_size("dp")
    team = TEAM
    tok, chans = key_gate.shape[1:]
    blocks = block_live.shape[1]
    qlen = tok // blocks
    prow = blocks * ctx
    qblocks = qlen // SUB
    share = chans // (ctx * team)
    width = 2 * team * share
    peers = team * ctx
    grid = (blocks, qlen, chans)
    halves = (2 * blocks * chans // min(chans, 128) * 2, qlen // 2, min(chans, 128))
    first, mid, back, last = transform_tables(prow, qlen)
    first, last = jnp.asarray(first), jnp.asarray(last)
    turns = jnp.asarray(np.concatenate([mid, back]))
    spread = jnp.asarray(spread_table(qblocks, 2 * team, share))
    order = np.arange(peers)
    random.Random(SEED).shuffle(order)
    seats = np.argsort(order).reshape(team, ctx).tolist()
    teams = [(start * ctx + order).tolist() for start in range(0, dp, team)]

    def trade(x, bit):
        return lax.ppermute(x, "dp", [(i, i ^ bit) for i in range(dp)])

    def exchange(x):
        return lax.all_to_all(
            x, ("dp", "ctx"), split_axis=0, concat_axis=0, tiled=True, axis_index_groups=teams
        )

    packed, key, value, cot = call(
        functools.partial(prep_kernel, team),
        [
            pltpu.with_memory_space_constraint(x, pltpu.HBM)
            for x in (
                block_live,
                out_gate.reshape(grid),
                key_gate.reshape(grid),
                value_input.reshape(grid),
                cotangent.reshape(grid),
                filter_taps.reshape(grid),
            )
        ],
        [shaped((peers, qlen + SUB, width))] + [shaped(grid)] * 3,
        scratch=[
            *[pltpu.VMEM(grid, BF16)] * 3,
            pltpu.VMEM((qlen, chans), BF16),
            pltpu.SMEM(block_live.shape, jnp.int32),
            pltpu.VMEM(halves, BF16),
            pltpu.VMEM((peers, SUB, width), F32),
            pltpu.SemaphoreType.DMA((10,)),
        ],
        in_specs=[FAR] * 6,
        name="gate_and_pack",
        flops=10**10,
    )
    tables = [first, spread, turns, last]
    outs = call(
        functools.partial(main_kernel, seats),
        [
            exchange(packed),
            *tables,
        ],
        [shaped((peers, qlen + 2 * SUB, width))],
        scratch=[
            pltpu.VMEM((qblocks, prow * SUB, 2 * width), BF16),
            pltpu.VMEM((prow * SUB, width), BF16),
            pltpu.VMEM((2 * prow, qlen, 2 * width), BF16),
            pltpu.VMEM((qblocks, 2 * prow * SUB, 2 * width), BF16),
            pltpu.VMEM((ctx * blocks, qlen, width), BF16),
            pltpu.VMEM((qblocks // 2 * blocks, ctx * 2 * SUB, width), BF16),
            pltpu.VMEM((qblocks // 2, prow * SUB, width), F32),
        ],
        name="convolve",
    )
    bit = team
    while bit < dp:
        part = outs[:, qlen:, :]
        total = part.astype(F32) + trade(part, bit).astype(F32)
        outs = lax.dynamic_update_slice(outs, total.astype(BF16), (0, qlen, 0))
        bit *= 2
    recv = exchange(outs)
    mine = recv[:, qlen:, :]
    theirs = trade(mine, 1)
    scale = 1.0 / math.sqrt(dp * tok * ctx)
    half = (blocks // 2, qlen, chans)
    *grads, begun = call(
        functools.partial(post_kernel, scale),
        [recv, key, value, cot],
        [shaped(grid)] * 4,
        scratch=[
            *[pltpu.VMEM(grid, BF16)] * 3,
            pltpu.VMEM(half, BF16),
            pltpu.VMEM(halves, BF16),
            pltpu.VMEM((peers, 2 * SUB, width), BF16),
            pltpu.SemaphoreType.DMA((7,)),
        ],
        out_specs=[FAR] * 4,
        name="ungate",
    )
    grad_taps = call(
        functools.partial(finish_kernel, scale),
        [theirs, pltpu.with_memory_space_constraint(begun, pltpu.HBM)],
        [shaped(grid)],
        scratch=[
            pltpu.VMEM(half, BF16),
            pltpu.VMEM((peers, 2 * SUB, width), BF16),
            pltpu.SemaphoreType.DMA((1,)),
        ],
        in_specs=[VM, FAR],
        out_specs=FAR,
        aliases={1: 0},
        name="scale_taps",
    )
    return (*[x.reshape(key_gate.shape) for x in grads], grad_taps.reshape(filter_taps.shape))


def solution(mesh):
    return jax.shard_map(
        local,
        mesh=mesh,
        in_specs=(
            P("dp", "ctx", None),
            P("dp", "ctx", None),
            P("dp", "ctx", None),
            P("ctx", None),
            P("dp", "ctx", None),
            P("dp", "ctx"),
        ),
        out_specs=(
            P("dp", "ctx", None),
            P("dp", "ctx", None),
            P("dp", "ctx", None),
            P("ctx", None),
        ),
        check_vma=False,
    )
```
